32 devices in a mesh: block: 1, tile: 32 (over z, y, x, core).
Axes of the slice: x: 2, y: 2, z: 4, core: 2. Of those that a mesh axis runs over, the one named last changes fastest.
Arguments:
- acts: bfloat16 [2, 32, 64, 384], P('block', 'tile'), may hold values from -6 to 6
- gamma: float32 [384], replicated, may hold values from 0.25 to 1.75
- beta: float32 [384], replicated, may hold values from -3 to 3
- weights: bfloat16 [384, 27, 192], P('tile'), may hold values from -0.0625 to 0.0625
- cotangent: bfloat16 [2, 64, 128, 192], P('block', 'tile'), may hold values from -6 to 6
Outputs:
- d_acts: bfloat16 [2, 32, 64, 384], P('block', 'tile')
- d_weights: float32 [384, 27, 192], P('tile')
The draws below stay inside these ranges and needn't reach their ends.
All inputs are finite; a program needn't handle non-finite values.
Results may differ from the reference program's by a relative error of at most 0.0029.
Values may be sent and summed in bfloat16 or wider, within the bound.
No kernel may reach another device: no remote copies, remote signals or barrier semaphores. Data moves between devices by JAX's collectives and lax.ppermute only.
A program may use at most 128 MiB of HBM per device.

```python
import jax
import jax.numpy as jnp
from jax import lax

C_IN = 384
C_OUT = 192
GROUPS = 32
TAPS = 27
WL = 64
FRAMES = 2
HEIGHT = 32


def block_levels(key, shape, pieces, least, largest):
    factor_of = 1.0
    for dim, blocks in pieces:
        draws = jax.random.uniform(jax.random.fold_in(jax.random.fold_in(key, 6), dim), (blocks,), jnp.float32, least / len(pieces), largest / len(pieces))
        factor_of = factor_of * jnp.repeat(jnp.exp(draws), shape[dim] // blocks).reshape((-1,) + (1,) * (len(shape) - 1 - dim))
    return factor_of


def noise(rng, shape, deviation, reach, cuts=(), kind=jnp.bfloat16):
    gain = block_levels(rng, shape, cuts, -0.22, 0.18) if cuts else 1.0
    array = jax.random.normal(rng, shape, jnp.float32) * deviation * gain
    return jnp.minimum(jnp.maximum(array, -reach), reach).astype(kind)


def setup_inputs(seed: int = 0) -> dict:
    seeds = jax.random.split(jax.random.key(seed), 6)
    acts = noise(seeds[0], (FRAMES, HEIGHT, WL, C_IN), 1.0, 6.0, ((1, 32),))
    gamma = jnp.clip(1.0 + 0.15 * jax.random.normal(seeds[1], (C_IN,), jnp.float32), 0.25, 1.75)
    beta = noise(seeds[2], (C_IN,), 0.5, 3.0, (), jnp.float32)
    weights = noise(seeds[3], (C_IN, TAPS, C_OUT), (27 * C_IN) ** -0.5, 0.0625, ((0, 32),))
    cotangent = noise(seeds[4], (FRAMES, 2 * HEIGHT, 2 * WL, C_OUT), 1.0, 6.0, ((1, 32),))
    return dict(acts=acts, gamma=gamma, beta=beta, weights=weights, cotangent=cotangent)


norm_eps = 1e-06

def group_totals(values, frames, per_group):
    return lax.optimization_barrier(jnp.sum(values, axis=(1, 2))).reshape(frames, GROUPS, per_group).sum(-1)

def reference(acts, gamma, beta, weights, cotangent):
    frames, height, width, channels = acts.shape
    per_group = channels // GROUPS
    group_size = height * width * per_group
    acts_wide = acts.astype(jnp.float32)
    stat_sum = group_totals(acts_wide, frames, per_group)
    stat_sq = group_totals(acts_wide * acts_wide, frames, per_group)
    group_mean = stat_sum / group_size
    inv_std = lax.rsqrt(stat_sq / group_size - group_mean * group_mean + norm_eps)
    mean_chan = jnp.repeat(group_mean, per_group, axis=1)[:, None, None, :]
    inv_chan = jnp.repeat(inv_std, per_group, axis=1)[:, None, None, :]
    normed = (acts_wide - mean_chan) * inv_chan
    shifted = normed * gamma + beta
    gate_value = jax.nn.sigmoid(shifted)
    hidden = (shifted * gate_value).astype(jnp.bfloat16)
    upsampled = jnp.repeat(jnp.repeat(hidden, 2, axis=1), 2, axis=2)
    upsampled = jnp.pad(upsampled, ((2, 0), (1, 1), (1, 1), (0, 0)))
    grad_field = jnp.pad(cotangent, ((0, 2), (1, 1), (1, 1), (0, 0)))
    up_rows = 2 * height
    up_cols = 2 * width
    num_cells = frames * up_rows * up_cols
    flat_grads = cotangent.reshape(num_cells, -1)
    act_grad = jnp.zeros((frames, height, width, channels), jnp.float32)
    weight_list = []
    for tap in range(27):
        tap_t = tap // 9
        tap_h = tap // 3 % 3
        tap_w = tap % 3
        window_g = grad_field[2 - tap_t:2 - tap_t + frames, 2 - tap_h:2 - tap_h + up_rows, 2 - tap_w:2 - tap_w + up_cols]
        window_g = window_g.reshape(num_cells, -1)
        back_grad = jnp.dot(window_g, weights[:, tap, :].T, preferred_element_type=jnp.float32)
        act_grad = act_grad + back_grad.reshape(frames, height, 2, width, 2, channels).sum(axis=(2, 4))
        window_h = upsampled[tap_t:tap_t + frames, tap_h:tap_h + up_rows, tap_w:tap_w + up_cols]
        window_h = window_h.reshape(num_cells, channels)
        weight_list.append(jnp.dot(window_h.T, flat_grads, preferred_element_type=jnp.float32))
    d_weights = jnp.stack(weight_list, 1)
    silu_slope = gate_value * (1.0 + shifted * (1.0 - gate_value))
    norm_grad = act_grad * silu_slope * gamma
    first_sum = group_totals(norm_grad, frames, per_group)
    second_sum = group_totals(norm_grad * normed, frames, per_group)
    first_chan = jnp.repeat(first_sum / group_size, per_group, axis=1)[:, None, None, :]
    second_chan = jnp.repeat(second_sum / group_size, per_group, axis=1)[:, None, None, :]
    d_acts = (inv_chan * (norm_grad - first_chan - normed * second_chan)).astype(jnp.bfloat16)
    return (d_acts, d_weights)
```

```python
import functools

import jax
import jax.numpy as jnp
from jax import lax
from jax.experimental import pallas as pl
from jax.experimental.pallas import tpu as pltpu
from jax.sharding import PartitionSpec as P

GROUPS = 32
norm_eps = 1e-06


F32 = jnp.float32
BF16 = jnp.bfloat16
SPLIT = 16


class Sizes:
    def __init__(self, acts, weights, cotangent, tiles, blocks):
        self.frames, low_rows, self.cols, self.chans = acts.shape
        self.taps, self.outs = weights.shape[1:]
        self.tiles, self.blocks = tiles, blocks
        self.inner = 1 << (tiles.bit_length() // 2)
        self.outer = tiles // self.inner
        self.pairs = self.inner // 2
        self.per = self.chans // GROUPS
        self.gp = 16
        self.rb = self.outer * self.gp
        self.cells = self.frames * self.cols
        self.wide = 2 * self.cols
        self.grad_frames = self.frames * (2 if blocks > 1 else 1)
        self.first = max(0, 3 - self.frames * blocks)
        self.used = 9 * (3 - self.first)
        self.half = (self.used + 1) // 2 * self.gp
        self.wrows = self.used * self.gp + self.half
        self.lo = 128
        self.hi = self.outs - self.lo
        self.count = float(low_rows * tiles * self.cols * self.per)
        self.edge_steps = [k for k in range(1, self.outer) if k & (k + 1) == 0]
        if low_rows != 1 or tiles != GROUPS or self.hi != 64 or self.outer > 8:
            raise ValueError("unsupported sizes")


def swap(value, mask):
    count = lax.axis_size("tile")
    return lax.ppermute(value, "tile", [(i, i ^ mask) for i in range(count)])


def place(g):
    me = lax.axis_index("tile")
    return lax.div(me, g.inner), lax.rem(me, g.inner)


def iota(shape, dim):
    return lax.broadcasted_iota(jnp.int32, shape, dim)


def dot(a, b, dims=((1,), (0,))):
    return lax.dot_general(a, b, (dims, ((), ())), preferred_element_type=F32)


def channel_select(g, w, count):
    shape = (count * g.rb, g.chans)
    row = iota(shape, 0)
    block = row >> (g.rb.bit_length() - 1)
    group = (row & (g.rb - 1)) >> 4
    lane = row & (g.gp - 1)
    chan = g.per * (g.inner * group + (w ^ block)) + lane
    return (chan == iota(shape, 1)) & (lane < g.per)


def column_select(g):
    shape = (g.cells, g.frames * 3 * g.wide)
    row, col = iota(shape, 0), iota(shape, 1)
    bits = g.wide.bit_length() - 1
    part = col >> bits
    frame, shift = part, part
    frame = (part >= 3).astype(jnp.int32)
    for f in range(2, g.frames):
        frame = frame + (part >= 3 * f).astype(jnp.int32)
    shift = part - 3 * frame
    low = ((col & (g.wide - 1)) + shift - 1) >> 1
    inside = (low >= 0) & (low < g.cols)
    return (inside & (low + frame * g.cols == row)).astype(BF16)


def split(value, parts):
    out = []
    for _ in range(parts):
        piece = value.astype(BF16)
        out.append(piece)
        value = value - piece.astype(F32)
    return out


def pack_acts_kernel(g, acts_ref, *out_refs):
    _, w = place(g)
    x = acts_ref[...].reshape(g.cells, g.chans)
    pick = channel_select(g, w, g.inner).astype(BF16)
    blocks = dot(pick, x, ((1,), (1,))).astype(BF16)
    for k, ref in enumerate(out_refs):
        ref[...] = blocks[2 * k * g.rb : 2 * (k + 1) * g.rb].reshape(2, g.rb, g.cells)


def pack_grads_kernel(g, grads_ref, out_ref):
    for t in range(g.grad_frames):
        for i in range(2):
            out_ref[3 * t + i] = grads_ref[t, i, :, : g.lo]
        out_ref[3 * t + 2] = jnp.concatenate(
            [grads_ref[t, i, :, g.lo :].astype(F32) for i in range(2)], axis=1
        ).astype(BF16)


def pack_rows(g, lo, hi):
    rest = hi[g.half :]
    if rest.shape[0] < g.half:
        rest = jnp.concatenate([rest, jnp.zeros((g.half - rest.shape[0], 128), F32)], axis=0)
    lane = iota((g.half, 128), 1)
    both = jnp.where(lane < 64, hi[: g.half], pltpu.roll(rest, 64, 1))
    return jnp.concatenate([lo, both], axis=0)


def unpack_hi(g, packed):
    lane = iota(packed.shape, 1)
    first = jnp.where(lane < 64, packed, 0.0)
    second = jnp.where(lane < 64, pltpu.roll(packed, 64, 1), 0.0)
    return jnp.concatenate([first, second], axis=0)[: g.used * g.gp]


def pack_weights_kernel(g, weights_ref, out_ref):
    rows = g.used * g.gp
    total = jnp.zeros((rows, g.outs), F32)
    row, tap = iota((rows, g.taps), 0), iota((rows, g.taps), 1)
    base = jnp.where(tap >= 9 * g.first, (tap - 9 * g.first) * g.gp, -g.gp)
    for i in range(g.per):
        total = total + dot((row == base + i).astype(BF16), weights_ref[i])
    hi = jnp.concatenate([total[:, g.lo :], jnp.zeros((rows, 64), F32)], axis=1)
    out_ref[...] = pack_rows(g, total[:, : g.lo], hi).astype(BF16)


def totals(g, first, second):
    pad = jnp.zeros((8 - g.outer, g.cells), F32)
    out = []
    for value in (first, second):
        out += [jnp.sum(value.reshape(g.outer, g.gp, g.cells), axis=1)]
        if g.outer < 8:
            out += [pad]
    return jnp.concatenate(out, axis=0)


def stats_kernel(g, *refs):
    direct, refs = refs[: g.pairs], refs[g.pairs :]
    crossed, refs = refs[: g.pairs], refs[g.pairs :]
    packed_ref, rows_ref, stats_ref, *sends = refs
    z, w = place(g)
    first = jnp.zeros((g.rb, g.cells), F32)
    second = jnp.zeros((g.rb, g.cells), F32)
    for k in range(g.pairs):
        for j, ref in enumerate((direct[k], crossed[k])):
            block = ref[j]
            rows_ref[w ^ (2 * k + j)] = block
            wide = block.astype(F32)
            first = first + wide
            second = second + wide * wide
    stats = totals(g, first, second)
    stats_ref[...] = stats
    pieces = split(stats, 3)
    for k, ref in enumerate(sends, 1):
        ref[: g.wrows] = packed_ref[...]
        for i, piece in enumerate(pieces):
            ref[g.wrows + i * SPLIT : g.wrows + (i + 1) * SPLIT] = piece
        if k in g.edge_steps:
            edge = jnp.where((z ^ k) == z + 1, g.inner - 1, 0)
            ref[g.wrows + 3 * SPLIT :] = rows_ref[edge]


def add_stats(g, own, received, start):
    for ref in received:
        for i in range(3):
            own = own + ref[start + i * SPLIT : start + (i + 1) * SPLIT].astype(F32)
    return own


def spread(g, stats):
    lane = iota((SPLIT, g.cells), 1)
    whole = jnp.zeros((SPLIT, g.cells), F32)
    for t in range(g.frames):
        mine = (lane >= t * g.cols) & (lane < (t + 1) * g.cols)
        part = jnp.sum(jnp.where(mine, stats, 0.0), axis=1, keepdims=True)
        whole = jnp.where(mine, part, whole)
    return tuple(
        jnp.concatenate(
            [
                jnp.broadcast_to(whole[s + q : s + q + 1], (g.gp, g.cells))
                for q in range(g.outer)
            ],
            axis=0,
        )
        for s in (0, 8)
    )


def main_kernel(g, *refs):
    refs = list(refs)
    take = lambda n: [refs.pop(0) for _ in range(n)]
    direct, crossed = take(g.pairs), take(g.pairs)
    rows_ref, stats_ref, packed_ref = take(3)
    received = take(g.outer - 1)
    gamma_ref, beta_ref = take(2)
    sends = take(g.outer - 1)
    own_ref, sums_ref, grad_ref, normed_ref, inv_ref = take(5)
    xs, wl, acc, hidden, slope, ups, field = refs
    z, w = place(g)
    rb, wide, frames = g.rb, g.wide, g.frames

    for k in range(g.pairs):
        for j, ref in enumerate((direct[k], crossed[k])):
            row = w ^ (2 * k + j)
            for t in range(g.grad_frames):
                both = ref[3 * t + 2]
                other = pltpu.roll(both.astype(F32), 64, 1).astype(BF16)
                for i, hi in enumerate((both, other)):
                    xs[t, row, i * wide : (i + 1) * wide, : g.lo] = ref[3 * t + i]
                    xs[t, row, i * wide : (i + 1) * wide, g.lo :] = hi

    for k in range(g.outer):
        ref = packed_ref if k == 0 else received[k - 1]
        rows = g.used * g.gp
        wl[:, z ^ k, :, : g.lo] = ref[:rows].reshape(g.used, g.gp, g.lo)
        hi = unpack_hi(g, ref[rows : g.wrows].astype(F32)).astype(BF16)
        wl[:, z ^ k, :, g.lo :] = hi.reshape(g.used, g.gp, 128)

    stats = add_stats(g, stats_ref[...], received, g.wrows)
    total, total_sq = spread(g, stats)
    mean = total / g.count
    inv = lax.rsqrt(total_sq / g.count - mean * mean + norm_eps)
    inv_ref[...] = inv
    pick = channel_select(g, w, 1)
    gamma = jnp.sum(jnp.where(pick, gamma_ref[...], 0.0), axis=1, keepdims=True)
    beta = jnp.sum(jnp.where(pick, beta_ref[...], 0.0), axis=1, keepdims=True)

    def activate(place_at, block, present):
        normed = (block.astype(F32) - mean) * inv
        shifted = normed * gamma + beta
        gate = jax.nn.sigmoid(shifted)
        normed_ref[place_at] = normed
        hidden[place_at] = (shifted * gate * present).astype(BF16)
        slope[place_at] = gate * (1.0 + shifted * (1.0 - gate)) * gamma * present

    for place_at, step in ((0, -1), (g.inner + 1, 1)):
        block = jnp.zeros((rb, g.cells), BF16)
        for k in g.edge_steps:
            at = g.wrows + 3 * SPLIT
            block = jnp.where((z ^ k) == z + step, received[k - 1][at : at + rb], block)
        inside = (z + step >= 0) & (z + step < g.outer)
        activate(place_at, block, jnp.where(inside, 1.0, 0.0))

    @pl.loop(0, g.inner)
    def _(i):
        activate(i + 1, rows_ref[i], 1.0)

    select = column_select(g)
    count = g.inner + 2
    ups[...] = (
        dot(hidden[...].reshape(count * rb, g.cells), select)
        .astype(BF16)
        .reshape(count, rb, frames * 3 * wide)
    )

    acc[...] = jnp.zeros_like(acc)
    field[...] = jnp.zeros_like(field)

    @pl.loop(0, g.inner)
    def _(i):
        for later in range(g.grad_frames):
            x = xs[later, i]
            for a in range(g.first, 3):
                t = later + a - 2
                if t < 0 or t >= frames:
                    continue
                taps = slice(9 * (a - g.first), 9 * (a - g.first + 1))
                lanes = [slice((3 * t + e) * wide, (3 * t + e + 1) * wide) for e in range(3)]
                pieces = []
                for upper, lower in ((0, 1), (1, 1), (1, 2)):
                    for e in range(3):
                        pieces.append(
                            jnp.concatenate(
                                [ups[i + upper, :, lanes[e]], ups[i + lower, :, lanes[e]]], axis=1
                            )
                        )
                terms = dot(jnp.concatenate(pieces, axis=0), x)
                acc[taps] += terms.reshape(9, g.outer, g.gp, 256)
                back = dot(wl[taps].reshape(9 * rb, 256), x, ((1,), (1,)))
                part = lambda b, e, fine: back[
                    (3 * b + e) * rb : (3 * b + e + 1) * rb, fine * wide : (fine + 1) * wide
                ]
                for e in range(3):
                    field[i, :, lanes[e]] += part(0, e, 0)
                    field[i + 1, :, lanes[e]] += (part(1, e, 0) + part(2, e, 0)) + (
                        part(0, e, 1) + part(1, e, 1)
                    )
                    field[i + 2, :, lanes[e]] += part(2, e, 1)

    flat = field[...].reshape(count * rb, frames * 3 * wide)
    pieces = split(flat, 2)
    act_grad = dot(pieces[0], select, ((1,), (1,))) + dot(pieces[1], select, ((1,), (1,)))
    grad = act_grad.reshape(count, rb, g.cells) * slope[...]
    grad_ref[...] = grad
    sums = totals(g, jnp.sum(grad, axis=0), jnp.sum(grad * normed_ref[...], axis=0))
    sums_ref[...] = sums

    own_ref[...] = acc[:, z].reshape(g.used * g.gp, 256)
    parts = split(sums, 3)
    for k, ref in enumerate(sends, 1):
        terms = acc[:, z ^ k].reshape(g.used * g.gp, 256)
        ref[: g.wrows] = pack_rows(g, terms[:, : g.lo], terms[:, g.lo :]).astype(BF16)
        for i, piece in enumerate(parts):
            ref[g.wrows + i * SPLIT : g.wrows + (i + 1) * SPLIT] = piece
        if k in g.edge_steps:
            edge = grad_ref[jnp.where((z ^ k) == z + 1, g.inner + 1, 0)]
            for i, piece in enumerate(split(edge, 2)):
                at = g.wrows + 3 * SPLIT + i * rb
                ref[at : at + rb] = piece


def finish_kernel(g, *refs):
    refs = list(refs)
    take = lambda n: [refs.pop(0) for _ in range(n)]
    sums_ref, grad_ref, normed_ref, inv_ref = take(4)
    received = take(g.outer - 1)
    sends = refs
    z, w = place(g)
    sums = add_stats(g, sums_ref[...], received, g.wrows)
    first, second = spread(g, sums)
    first, second = first / g.count, second / g.count
    inv = inv_ref[...]
    edges = []
    for step in (-1, 1):
        edge = jnp.zeros((g.rb, g.cells), F32)
        for k in g.edge_steps:
            at = g.wrows + 3 * SPLIT
            value = received[k - 1][at : at + g.rb].astype(F32)
            value = value + received[k - 1][at + g.rb : at + 2 * g.rb].astype(F32)
            edge = jnp.where((z ^ k) == z + step, value, edge)
        edges.append(edge)
    for k, ref in enumerate(sends):
        for j in range(2):
            row = w ^ (2 * k + j)
            grad = grad_ref[row + 1]
            grad = grad + jnp.where(row == 0, edges[0], 0.0)
            grad = grad + jnp.where(row == g.inner - 1, edges[1], 0.0)
            ref[j] = (inv * (grad - first - normed_ref[row + 1] * second)).astype(BF16)


def unpack_acts_kernel(g, *refs):
    direct, crossed, out_ref = refs[: g.pairs], refs[g.pairs : 2 * g.pairs], refs[-1]
    _, w = place(g)
    pick = channel_select(g, w, g.inner).astype(BF16)
    blocks = []
    for k in range(g.pairs):
        blocks += [direct[k][0], crossed[k][1]]
    out = dot(jnp.concatenate(blocks, axis=0), pick, ((0,), (0,)))
    out_ref[...] = out.astype(BF16).reshape(out_ref.shape)


def unpack_weights_kernel(g, own_ref, *refs):
    *received, out_ref, low, high = refs
    rows = g.used * g.gp
    lo = own_ref[:, : g.lo]
    hi = jnp.zeros((g.half, 128), F32)
    for ref in received:
        lo = lo + ref[:rows].astype(F32)
        hi = hi + ref[rows : g.wrows].astype(F32)
    low[...] = lo
    high[...] = own_ref[:, g.lo :] + unpack_hi(g, hi)
    for i in range(g.per):
        at = pl.ds(i, g.used, stride=g.gp)
        if g.first:
            out_ref[i, : 9 * g.first, :] = jnp.zeros((9 * g.first, g.outs), F32)
        out_ref[i, 9 * g.first :, : g.lo] = low[at, :]
        out_ref[i, 9 * g.first :, g.lo :] = high[at, :][:, : g.hi]


def call(g, kernel, name, outs, args, scratch=(), flops=0):
    shapes = [jax.ShapeDtypeStruct(shape, kind) for shape, kind in outs]
    whole = pl.BlockSpec(memory_space=pltpu.VMEM)
    moved = sum(a.size * a.dtype.itemsize for a in list(args) + shapes)
    return pl.pallas_call(
        functools.partial(kernel, g),
        out_shape=shapes,
        in_specs=[whole] * len(args),
        out_specs=[whole] * len(shapes),
        scratch_shapes=list(scratch),
        compiler_params=pltpu.CompilerParams(vmem_limit_bytes=48 * 1024 * 1024),
        cost_estimate=pl.CostEstimate(flops=flops, bytes_accessed=moved, transcendentals=0),
        name=name,
    )(*args)


def shards(acts, gamma, beta, weights, cotangent):
    g = Sizes(acts, weights, cotangent, lax.axis_size("tile"), lax.axis_size("block"))
    if g.blocks > 1:
        pairs = [(i + 1, i) for i in range(g.blocks - 1)]
        following = lax.ppermute(cotangent, "block", pairs)
        cotangent = jnp.concatenate([cotangent, following], 0)
    block = ((2, g.rb, g.cells), BF16)
    sends = call(g, pack_acts_kernel, "pack_acts", [block] * g.pairs, [acts])
    acts_direct = [sends[0]] + [swap(sends[k], 2 * k) for k in range(1, g.pairs)]

    grads_shape = ((3 * g.grad_frames, g.wide, 128), BF16)
    (packed_grads,) = call(g, pack_grads_kernel, "pack_grads", [grads_shape], [cotangent])
    grads_direct = [packed_grads] + [swap(packed_grads, 2 * k) for k in range(1, g.pairs)]

    acts_crossed = [swap(v, 1) for v in acts_direct]
    (packed,) = call(
        g, pack_weights_kernel, "pack_weights", [((g.wrows, 128), BF16)], [weights]
    )

    stats_shape = ((SPLIT, g.cells), F32)
    steps = range(1, g.outer)
    extra = [g.rb if k in g.edge_steps else 0 for k in steps]
    rows, stats, *sends = call(
        g,
        stats_kernel,
        "stats",
        [((g.inner, g.rb, g.cells), BF16), stats_shape]
        + [((g.wrows + 3 * SPLIT + n, 128), BF16) for n in extra],
        acts_direct + acts_crossed + [packed],
    )
    received = [swap(v, g.inner * k) for k, v in zip(steps, sends)]
    grads_crossed = [swap(v, 1) for v in grads_direct]

    count = g.inner + 2
    outs = [((g.wrows + 3 * SPLIT + 2 * n, 128), BF16) for n in extra]
    outs += [((g.used * g.gp, 256), F32), stats_shape]
    outs += [((count, g.rb, g.cells), F32)] * 2 + [((g.rb, g.cells), F32)]
    scratch = [
        pltpu.VMEM((g.grad_frames, g.inner, 2 * g.wide, 256), BF16),
        pltpu.VMEM((g.used, g.outer, g.gp, 256), BF16),
        pltpu.VMEM((g.used, g.outer, g.gp, 256), F32),
        pltpu.VMEM((count, g.rb, g.cells), BF16),
        pltpu.VMEM((count, g.rb, g.cells), F32),
        pltpu.VMEM((count, g.rb, g.frames * 3 * g.wide), BF16),
        pltpu.VMEM((count, g.rb, g.frames * 3 * g.wide), F32),
    ]
    *sends, own, sums, grad, normed, inv = call(
        g,
        main_kernel,
        "main",
        outs,
        grads_direct
        + grads_crossed
        + [rows, stats, packed]
        + received
        + [gamma.reshape(1, -1), beta.reshape(1, -1)],
        scratch,
        flops=2 * 4 * g.inner * 9 * g.rb * 256 * 256 * g.grad_frames,
    )
    received = [swap(v, g.inner * k) for k, v in zip(steps, sends)]
    sends = call(
        g, finish_kernel, "finish", [block] * g.pairs, [sums, grad, normed, inv] + received
    )
    direct = [sends[0]] + [swap(sends[k], 2 * k) for k in range(1, g.pairs)]
    crossed = [swap(v, 1) for v in direct]
    (d_acts,) = call(
        g, unpack_acts_kernel, "unpack_acts", [(acts.shape, BF16)], direct + crossed
    )
    (d_weights,) = call(
        g,
        unpack_weights_kernel,
        "unpack_weights",
        [(weights.shape, F32)],
        [own] + received,
        [pltpu.VMEM((g.used * g.gp, 128), F32)] * 2,
    )
    if g.blocks > 1:
        d_weights = lax.psum(d_weights, "block")
    return (d_acts, d_weights)


def solution(mesh):
    placed = (
        P("block", "tile", None, None),
        P(),
        P(),
        P("tile", None, None),
        P("block", "tile", None, None),
    )
    return jax.shard_map(
        shards,
        mesh=mesh,
        in_specs=placed,
        out_specs=(P("block", "tile", None, None), P("tile", None, None)),
        check_vma=False,
    )
```

```python
import jax
import jax.numpy as jnp
from jax import lax
from jax.experimental import pallas as pl
from jax.experimental.pallas import tpu as pltpu
from jax.sharding import PartitionSpec as P

GROUPS = 32
norm_eps = 1e-06


F32 = jnp.float32
BF16 = jnp.bfloat16
SPLIT = 16


class Sizes:
    def __init__(self, acts, weights, cotangent, tiles, blocks):
        self.frames, low_rows, self.cols, self.chans = acts.shape
        self.taps, self.outs = weights.shape[1:]
        self.tiles, self.blocks = tiles, blocks
        self.inner = 1 << (tiles.bit_length() // 2)
        self.outer = tiles // self.inner
        self.pairs = self.inner // 2
        self.per = self.chans // GROUPS
        self.gp = 16
        self.rb = self.outer * self.gp
        self.cells = self.frames * self.cols
        self.wide = 2 * self.cols
        self.grad_frames = self.frames * (2 if blocks > 1 else 1)
        self.first = max(0, 3 - self.frames * blocks)
        self.used = 9 * (3 - self.first)
        self.half = -(-self.used * self.per // 32) * 16
        self.sent = 2 * self.half
        self.wrows = self.sent + self.half
        self.lo = 128
        self.hi = self.outs - self.lo
        self.order = [*range(1, self.outer, 2), *range(0, self.outer, 2)]
        self.grows = 2 * self.grad_frames * self.outs
        self.count = float(low_rows * tiles * self.cols * self.per)
        self.steps = [k for k in range(1, self.outer) if k & (k + 1) == 0]
        if low_rows != 1 or tiles != GROUPS or self.hi != 64 or self.outer > 8:
            raise ValueError("unsupported sizes")


def swap(value, mask):
    count = lax.axis_size("tile")
    return lax.ppermute(value, "tile", [(i, i ^ mask) for i in range(count)])


def place(g):
    me = lax.axis_index("tile")
    return lax.div(me, g.inner), lax.rem(me, g.inner)


def iota(shape, dim):
    return lax.broadcasted_iota(jnp.int32, shape, dim)


def dot(a, b, dims=((1,), (0,))):
    return lax.dot_general(a, b, (dims, ((), ())), preferred_element_type=F32)


def channel_select(g, w, count):
    shape = (count * g.rb, g.chans)
    row = iota(shape, 0)
    block = row >> (g.rb.bit_length() - 1)
    group = (row & (g.rb - 1)) >> 4
    lane = row & (g.gp - 1)
    chan = g.per * (g.inner * group + (w ^ block)) + lane
    return (chan == iota(shape, 1)) & (lane < g.per)


def column_select(g):
    shape = (g.cells, g.frames * 3 * g.wide)
    row, col = iota(shape, 0), iota(shape, 1)
    bits = g.wide.bit_length() - 1
    part = col >> bits
    frame, shift = part, part
    frame = (part >= 3).astype(jnp.int32)
    for f in range(2, g.frames):
        frame = frame + (part >= 3 * f).astype(jnp.int32)
    shift = part - 3 * frame
    low = ((col & (g.wide - 1)) + shift - 1) >> 1
    inside = (low >= 0) & (low < g.cols)
    return (inside & (low + frame * g.cols == row)).astype(BF16)


def split(value, parts):
    out = []
    for _ in range(parts):
        piece = value.astype(BF16)
        out.append(piece)
        value = value - piece.astype(F32)
    return out


def sort_acts_kernel(g, acts_ref, out_ref):
    _, w = place(g)
    pick = channel_select(g, w, g.inner).astype(BF16)
    out_ref[...] = dot(pick, acts_ref[...], ((1,), (1,))).astype(BF16)


def pack_kernel(g, blocks_ref, grads_ref, *out_refs):
    for k, ref in enumerate(out_refs):
        ref[: g.grows] = grads_ref[...]
        ref[g.grows :] = blocks_ref[2 * k * g.rb : 2 * (k + 1) * g.rb]


def pack_rows(g, value):
    hi = jnp.concatenate([value[:, g.lo :], jnp.zeros((g.sent, 64), F32)], axis=1)
    lane = iota((g.half, 128), 1)
    both = jnp.where(lane < 64, hi[: g.half], pltpu.roll(hi[g.half :], 64, 1))
    return jnp.concatenate([value[:, : g.lo], both], axis=0).astype(BF16)


def unpack_rows(g, packed):
    both = packed[g.sent :].astype(F32)
    lane = iota(both.shape, 1)
    first = jnp.where(lane < 64, both, 0.0)
    second = jnp.where(lane < 64, pltpu.roll(both, 64, 1), 0.0)
    hi = jnp.concatenate([first, second], axis=0).astype(BF16)
    return jnp.concatenate([packed[: g.sent], hi], axis=1)


def pack_weights_kernel(g, weights_ref, out_ref):
    total = jnp.zeros((g.sent, g.outs), F32)
    row, tap = iota((g.sent, g.taps), 0), iota((g.sent, g.taps), 1) - 9 * g.first
    for i in range(g.per):
        pick = (row == tap * g.per + i) & (tap >= 0)
        total = total + dot(pick.astype(BF16), weights_ref[i])
    out_ref[...] = pack_rows(g, total)


def totals(g, first, second):
    pad = jnp.zeros((8 - g.outer, g.cells), F32)
    out = []
    for value in (first, second):
        out += [jnp.sum(value.reshape(g.outer, g.gp, g.cells), axis=1)]
        if g.outer < 8:
            out += [pad]
    return jnp.concatenate(out, axis=0)


def send_stats(g, refs, stats, z, rows_ref, parts):
    pieces = split(stats, 3)
    last = rows_ref.shape[0] - 1
    for k, ref in enumerate(refs, 1):
        for i, piece in enumerate(pieces):
            ref[i * SPLIT : (i + 1) * SPLIT] = piece
        if k in g.steps:
            edge = rows_ref[jnp.where((z ^ k) == z + 1, last, 0)]
            for i, piece in enumerate(split(edge, parts) if parts > 1 else [edge]):
                ref[3 * SPLIT + i * g.rb : 3 * SPLIT + (i + 1) * g.rb] = piece


def stats_kernel(g, *refs):
    direct, crossed, refs = refs[: g.pairs], refs[g.pairs : 2 * g.pairs], refs[2 * g.pairs :]
    rows_ref, stats_ref, *sends = refs
    z, w = place(g)
    first = jnp.zeros((g.rb, g.cells), F32)
    second = jnp.zeros((g.rb, g.cells), F32)
    for k in range(g.pairs):
        for j, ref in enumerate((direct[k], crossed[k])):
            block = ref[g.grows + j * g.rb : g.grows + (j + 1) * g.rb]
            rows_ref[w ^ (2 * k + j)] = block
            wide = block.astype(F32)
            first = first + wide
            second = second + wide * wide
    stats = totals(g, first, second)
    stats_ref[...] = stats
    send_stats(g, sends, stats, z, rows_ref, 1)


def add_stats(own, received):
    for ref in received:
        for i in range(3):
            own = own + ref[i * SPLIT : (i + 1) * SPLIT].astype(F32)
    return own


def spread(g, stats):
    lane = iota((SPLIT, g.cells), 1)
    whole = jnp.zeros((SPLIT, g.cells), F32)
    for t in range(g.frames):
        mine = (lane >= t * g.cols) & (lane < (t + 1) * g.cols)
        part = jnp.sum(jnp.where(mine, stats, 0.0), axis=1, keepdims=True)
        whole = jnp.where(mine, part, whole)
    return tuple(
        jnp.concatenate(
            [
                jnp.broadcast_to(whole[s + q : s + q + 1], (g.gp, g.cells))
                for q in range(g.outer)
            ],
            axis=0,
        )
        for s in (0, 8)
    )


def prepare_weights_kernel(g, *refs):
    *packed, out_ref = refs
    z, _ = place(g)
    shape = (g.used * g.gp, g.sent)
    row, col = iota(shape, 0), iota(shape, 1)
    tap, lane = row >> 4, row & (g.gp - 1)
    pick = ((col == tap * g.per + lane) & (lane < g.per)).astype(BF16)
    blocks = [(ref, at) for ref in packed for at in range(0, ref.shape[0], g.wrows)]
    for k, (ref, at) in enumerate(blocks):
        value = dot(pick, unpack_rows(g, ref[at : at + g.wrows])).astype(BF16)
        out_ref[:, z ^ k] = value.reshape(g.used, g.gp, 256)


def meetings(g, later):
    pairs = [(a, later + a - 2) for a in range(g.first, 3)]
    return [(a, t) for a, t in pairs if 0 <= t < g.frames]


def fine_rows(g, ref, later):
    at = 2 * later * g.outs
    return jnp.concatenate([ref[at : at + g.outs], ref[at + g.outs : at + 2 * g.outs]], axis=1)


def lanes_of(g, t, e):
    return slice((3 * t + e) * g.wide, (3 * t + e + 1) * g.wide)


def field_kernel(g, *refs):
    direct, crossed, refs = refs[: g.pairs], refs[g.pairs : 2 * g.pairs], refs[2 * g.pairs :]
    weights_ref, field = refs
    _, w = place(g)
    rb, wide = g.rb, g.wide
    field[...] = jnp.zeros_like(field)
    for k in range(g.pairs):
        for j, ref in enumerate((direct[k], crossed[k])):
            row = w ^ (2 * k + j)
            for later in range(g.grad_frames):
                pairs = meetings(g, later)
                if not pairs:
                    continue
                low, high = pairs[0][0] - g.first, pairs[-1][0] - g.first + 1
                taps = weights_ref[9 * low : 9 * high].reshape(9 * (high - low) * rb, 256)
                every = dot(taps[:, : g.outs], fine_rows(g, ref, later))
                for n, (_, t) in enumerate(pairs):
                    back = every[9 * n * rb : 9 * (n + 1) * rb]
                    part = lambda b, e, fine: back[
                        (3 * b + e) * rb : (3 * b + e + 1) * rb, fine * wide : (fine + 1) * wide
                    ]
                    for e in range(3):
                        lanes = lanes_of(g, t, e)
                        field[row, :, lanes] += part(0, e, 0)
                        field[row + 1, :, lanes] += (part(1, e, 0) + part(2, e, 0)) + (
                            part(0, e, 1) + part(1, e, 1)
                        )
                        field[row + 2, :, lanes] += part(2, e, 1)


def norm_grad_kernel(g, *refs):
    rows_ref, stats_ref, gamma_ref, beta_ref, field_ref, *refs = refs
    received, refs = refs[: g.outer - 1], refs[g.outer - 1 :]
    normed_ref, hidden_ref, inv_ref, sums_ref, grad_ref, *sends, slope_ref, hidden_scratch = refs
    z, w = place(g)
    rb = g.rb
    total, total_sq = spread(g, add_stats(stats_ref[...], received))
    mean = total / g.count
    inv = lax.rsqrt(total_sq / g.count - mean * mean + norm_eps)
    inv_ref[...] = inv
    pick = channel_select(g, w, 1)
    gamma = jnp.sum(jnp.where(pick, gamma_ref[...].reshape(1, g.chans), 0.0), axis=1, keepdims=True)
    beta = jnp.sum(jnp.where(pick, beta_ref[...].reshape(1, g.chans), 0.0), axis=1, keepdims=True)

    def activate(place_at, block, present):
        normed = (block.astype(F32) - mean) * inv
        shifted = normed * gamma + beta
        gate = jax.nn.sigmoid(shifted)
        normed_ref[place_at] = normed
        hidden = (shifted * gate * present).astype(BF16).reshape(g.outer, g.gp, g.cells)
        hidden_scratch[...] = hidden
        for at, k in enumerate(g.order):
            hidden_ref[at, place_at] = hidden_scratch[z ^ k]
        slope_ref[place_at] = gate * (1.0 + shifted * (1.0 - gate)) * gamma * present

    for place_at, step in ((0, -1), (g.inner + 1, 1)):
        block = jnp.zeros((rb, g.cells), BF16)
        for k in g.steps:
            edge = received[k - 1][3 * SPLIT : 3 * SPLIT + rb]
            block = jnp.where((z ^ k) == z + step, edge, block)
        inside = (z + step >= 0) & (z + step < g.outer)
        activate(place_at, block, jnp.where(inside, 1.0, 0.0))

    @pl.loop(0, g.inner)
    def _(i):
        activate(i + 1, rows_ref[i], 1.0)

    count = g.inner + 2
    select = column_select(g)
    flat = field_ref[...].reshape(count * rb, g.frames * 3 * g.wide)
    pieces = split(flat, 2)
    act_grad = dot(pieces[0], select, ((1,), (1,))) + dot(pieces[1], select, ((1,), (1,)))
    grad = act_grad.reshape(count, rb, g.cells) * slope_ref[...]
    grad_ref[...] = grad
    sums = totals(g, jnp.sum(grad, axis=0), jnp.sum(grad * normed_ref[...], axis=0))
    sums_ref[...] = sums
    send_stats(g, sends, sums, z, grad_ref, 2)


def kernel_terms(g, first, direct, crossed, hidden_ref, acc, ups):
    _, w = place(g)
    part = acc.shape[0]
    flat = hidden_ref[first : first + part].reshape(-1, g.cells)
    ups[...] = dot(flat, column_select(g)).astype(BF16).reshape(ups.shape)
    started = set()
    for later in range(g.grad_frames):
        for a, t in meetings(g, later):
            left, right = [], []
            for k in range(g.pairs):
                for j, ref in enumerate((direct[k], crossed[k])):
                    row = w ^ (2 * k + j)
                    pieces = []
                    for group in range(part):
                        for upper, lower in ((0, 1), (1, 1), (1, 2)):
                            for e in range(3):
                                lanes = lanes_of(g, t, e)
                                sides = [ups[group, row + at, :, lanes] for at in (upper, lower)]
                                pieces.append(jnp.concatenate(sides, axis=1))
                    left.append(jnp.concatenate(pieces, axis=0))
                    right.append(fine_rows(g, ref, later))
            terms = dot(
                jnp.concatenate(left, axis=1), jnp.concatenate(right, axis=1), ((1,), (1,))
            ).reshape(part, 9, g.gp, g.outs)
            taps = slice(9 * (a - g.first), 9 * (a - g.first + 1))
            if a in started:
                acc[:, taps] += terms
            else:
                acc[:, taps] = terms
                started.add(a)


def sent_order(g):
    shape = (g.sent, g.used * g.gp)
    row, col = iota(shape, 0), iota(shape, 1)
    tap, lane = col >> 4, col & (g.gp - 1)
    return ((row == tap * g.per + lane) & (lane < g.per)).astype(BF16)


def sent_terms_kernel(g, *refs):
    direct, crossed, refs = refs[: g.pairs], refs[g.pairs : 2 * g.pairs], refs[2 * g.pairs :]
    hidden_ref, send_ref, acc, ups = refs
    kernel_terms(g, 0, direct, crossed, hidden_ref, acc, ups)
    pick = sent_order(g)
    for i in range(g.outer // 2):
        terms = acc[i].reshape(g.used * g.gp, g.outs).astype(BF16)
        send_ref[i * g.wrows : (i + 1) * g.wrows] = pack_rows(g, dot(pick, terms))


def kept_terms_kernel(g, *refs):
    direct, crossed, refs = refs[: g.pairs], refs[g.pairs : 2 * g.pairs], refs[2 * g.pairs :]
    hidden_ref, own_ref, *kept, acc, ups = refs
    kernel_terms(g, g.outer // 2, direct, crossed, hidden_ref, acc, ups)
    own_ref[...] = acc[0].reshape(g.used * g.gp, g.outs)
    pick = sent_order(g)
    for i in range(1, g.outer // 2):
        terms = acc[i].reshape(g.used * g.gp, g.outs)
        kept[0][i - 1] = sum(dot(pick, piece) for piece in split(terms, 2))


def halve_kernel(g, bit, keep_ref, received_ref, *refs):
    send_ref, *kept = refs
    for i in range(keep_ref.shape[0]):
        block = received_ref[(i + 1) * g.wrows : (i + 2) * g.wrows]
        total = keep_ref[i] + unpack_rows(g, block).astype(F32)[:, : g.outs]
        if i % 2:
            kept[0][i // 2] = total
        else:
            send_ref[i // 2 * g.wrows : (i // 2 + 1) * g.wrows] = pack_rows(g, total)


def finish_kernel(g, *refs):
    sums_ref, grad_ref, normed_ref, inv_ref, *refs = refs
    received, sends = refs[: g.outer - 1], refs[g.outer - 1 :]
    z, w = place(g)
    first, second = spread(g, add_stats(sums_ref[...], received))
    first, second = first / g.count, second / g.count
    inv = inv_ref[...]
    edges = []
    for step in (-1, 1):
        edge = jnp.zeros((g.rb, g.cells), F32)
        for k in g.steps:
            ref, at = received[k - 1], 3 * SPLIT
            value = ref[at : at + g.rb].astype(F32) + ref[at + g.rb :].astype(F32)
            edge = jnp.where((z ^ k) == z + step, value, edge)
        edges.append(edge)
    for k, ref in enumerate(sends):
        for j in range(2):
            row = w ^ (2 * k + j)
            grad = grad_ref[row + 1]
            grad = grad + jnp.where(row == 0, edges[0], 0.0)
            grad = grad + jnp.where(row == g.inner - 1, edges[1], 0.0)
            ref[j] = (inv * (grad - first - normed_ref[row + 1] * second)).astype(BF16)


def unpack_kernel(g, own_ref, *refs):
    steps = g.outer.bit_length() - 1
    received, refs = refs[:steps], refs[steps:]
    direct, (crossed, acts_ref, out_ref, low, high) = refs[: g.pairs], refs[g.pairs :]
    _, w = place(g)
    pick = channel_select(g, w, g.inner).astype(BF16)
    blocks = []
    for k in range(g.pairs):
        blocks += [direct[k][0], crossed[k]]
    d_acts = dot(jnp.concatenate(blocks, axis=0), pick, ((0,), (0,)))
    acts_ref[...] = d_acts.astype(BF16).reshape(acts_ref.shape)

    step = 32
    shape = (g.per * step, g.sent)
    row, col = iota(shape, 0), iota(shape, 1)
    tap, lane = row & (step - 1), row >> 5
    pick = ((col == tap * g.per + lane) & (tap < g.used)).astype(BF16)
    total = jnp.zeros((g.per * step, 256), F32)
    for ref in received:
        total = total + dot(pick, unpack_rows(g, ref[: g.wrows]))
    low[...] = own_ref[:, : g.lo]
    high[:, : g.hi] = own_ref[:, g.lo :]
    for i in range(g.per):
        at = pl.ds(i, g.used, stride=g.gp)
        there = total[i * step : i * step + g.used]
        if g.first:
            out_ref[i, : 9 * g.first, :] = jnp.zeros((9 * g.first, g.outs), F32)
        out_ref[i, 9 * g.first :, : g.lo] = low[at, :] + there[:, : g.lo]
        out_ref[i, 9 * g.first :, g.lo :] = high[at, :][:, : g.hi] + there[:, g.lo : g.outs]


def call(g, kernel, name, outs, args, scratch=(), flops=0, after=()):
    shapes = [jax.ShapeDtypeStruct(shape, kind) for shape, kind in outs]
    whole = pl.BlockSpec(memory_space=pltpu.VMEM)
    moved = sum(a.size * a.dtype.itemsize for a in list(args) + shapes)
    count = len(args)
    rest = count + len(after)
    return pl.pallas_call(
        lambda *refs: kernel(g, *refs[:count], *refs[rest:]),
        out_shape=shapes,
        in_specs=[whole] * count + [pl.BlockSpec(memory_space=pl.ANY)] * len(after),
        out_specs=[whole] * len(shapes),
        scratch_shapes=list(scratch),
        compiler_params=pltpu.CompilerParams(vmem_limit_bytes=48 * 1024 * 1024),
        cost_estimate=pl.CostEstimate(flops=flops, bytes_accessed=moved, transcendentals=0),
        name=name,
    )(*args, *after)


def copy_kernel(g, in_ref, out_ref):
    out_ref[...] = in_ref[...]


def join_kernel(g, *refs):
    *parts, out_ref = refs
    at = 0
    for ref in parts:
        out_ref[at : at + ref.shape[0]] = ref[...]
        at += ref.shape[0]


def cross_kernel(g, *refs):
    *blocks, out_ref = refs
    for k, ref in enumerate(blocks):
        out_ref[k] = ref[1]


def cross(g, name, direct):
    shape = (g.pairs, g.rb, g.cells)
    (out,) = call(g, cross_kernel, name, [(shape, BF16)], direct)
    return swap(out, 1)


def shards(acts, gamma, beta, weights, cotangent):
    g = Sizes(acts, weights, cotangent, lax.axis_size("tile"), lax.axis_size("block"))
    if g.blocks > 1:
        pairs = [(i + 1, i) for i in range(g.blocks - 1)]
        following = lax.ppermute(cotangent, "block", pairs)
        cotangent = jnp.concatenate([cotangent, following], 0)
    count = g.inner + 2
    block = ((2, g.rb, g.cells), BF16)
    rows_shape = ((count, g.rb, g.cells), F32)
    stats_shape = ((SPLIT, g.cells), F32)
    packed_shape = ((g.wrows, 128), BF16)
    wide_shape = (count, g.rb, g.frames * 3 * g.wide)
    over_z = lambda values: [swap(v, g.inner * k) for k, v in enumerate(values, 1)]
    sums_shapes = lambda parts: [
        ((3 * SPLIT + (parts * g.rb if k in g.steps else 0), 128), BF16)
        for k in range(1, g.outer)
    ]

    packed = list(
        call(g, pack_weights_kernel, "pack_weights", [packed_shape], [weights], flops=6 * 10**9)
    )
    for bit in range(g.outer.bit_length() - 1):
        whole = packed[0]
        if bit:
            shape = ((g.wrows << bit, 128), BF16)
            (whole,) = call(g, join_kernel, "join_kernel_rows", [shape], packed)
        packed.append(swap(whole, g.inner << bit))
    (blocks,) = call(
        g,
        sort_acts_kernel,
        "sort_acts",
        [((g.inner * g.rb, g.cells), BF16)],
        [acts.reshape(g.cells, g.chans)],
        flops=6 * 10**9,
    )
    sends = call(
        g,
        pack_kernel,
        "pack",
        [((g.grows + 2 * g.rb, g.cells), BF16)] * g.pairs,
        [blocks, jnp.swapaxes(cotangent, 2, 3).reshape(g.grows, g.wide)],
    )
    direct = [sends[0]] + [swap(sends[k], 2 * k) for k in range(1, g.pairs)]
    (last,) = call(
        g, copy_kernel, "pass_on", [(sends[0].shape, BF16)], direct[-1:], after=packed[1:]
    )
    arrived = direct + [swap(v, 1) for v in direct[:-1] + [last]]
    rows, stats, *sends = call(
        g,
        stats_kernel,
        "stats",
        [((g.inner, g.rb, g.cells), BF16), stats_shape] + sums_shapes(1),
        arrived,
    )
    received = over_z(sends)
    kernel_shape = ((g.used, g.outer, g.gp, 256), BF16)
    (rows_of_kernel,) = call(g, prepare_weights_kernel, "kernel_rows", [kernel_shape], packed)
    flops = 2 * 2 * g.inner * 9 * g.rb * 256 * 256 * g.grad_frames
    (field,) = call(
        g, field_kernel, "field_grad", [(wide_shape, F32)], arrived + [rows_of_kernel], flops=flops
    )
    hidden_shape = ((g.outer, count, g.gp, g.cells), BF16)
    normed, hidden, inv, sums, grad, *sends = call(
        g,
        norm_grad_kernel,
        "norm_grad",
        [rows_shape, hidden_shape, ((g.rb, g.cells), F32), stats_shape, rows_shape]
        + sums_shapes(2),
        [rows, stats, gamma, beta, field] + received,
        [pltpu.VMEM(*rows_shape), pltpu.VMEM((g.outer, g.gp, g.cells), BF16)],
    )
    received = over_z(sends)
    half = g.outer // 2
    kept_shape = lambda count: [((count, g.sent, g.outs), F32)] if count else []
    scratch = [
        pltpu.VMEM((half, g.used, g.gp, g.outs), F32),
        pltpu.VMEM((half, count, g.gp, wide_shape[-1]), BF16),
    ]
    (send,) = call(
        g,
        sent_terms_kernel,
        "sent_terms",
        [((half * g.wrows, 128), BF16)],
        arrived + [hidden],
        scratch,
        flops // 2,
    )
    (send,) = call(g, copy_kernel, "pass_terms", [(send.shape, BF16)], [send], after=received)
    terms = [swap(send, g.inner)]
    sends = call(
        g,
        finish_kernel,
        "finish",
        [block] * g.pairs,
        [sums, grad, normed, inv] + received,
        after=[send],
    )
    direct = [sends[0]] + [swap(sends[k], 2 * k) for k in range(1, g.pairs)]
    own, *kept = call(
        g,
        kept_terms_kernel,
        "kept_terms",
        [((g.used * g.gp, g.outs), F32)] + kept_shape(half - 1),
        arrived + [hidden],
        scratch,
        flops // 2,
        after=sends[:1],
    )
    bit = 1
    while kept:
        half //= 2
        send, *kept = call(
            g,
            lambda g, *refs, bit=bit: halve_kernel(g, bit, *refs),
            "halve",
            [((half * g.wrows, 128), BF16)] + kept_shape(half - 1),
            [kept[0], terms[-1]],
            after=direct[1:2],
        )
        terms.append(swap(send, g.inner << bit))
        bit += 1
    crossed = cross(g, "cross_grads", direct)
    d_acts, d_weights = call(
        g,
        unpack_kernel,
        "unpack",
        [(acts.shape, BF16), (weights.shape, F32)],
        [own] + terms + direct + [crossed],
        [pltpu.VMEM((g.used * g.gp, 128), F32)] * 2,
    )
    if g.blocks > 1:
        d_weights = lax.psum(d_weights, "block")
    return (d_acts, d_weights)


def solution(mesh):
    placed = (
        P("block", "tile", None, None),
        P(),
        P(),
        P("tile", None, None),
        P("block", "tile", None, None),
    )
    return jax.shard_map(
        shards,
        mesh=mesh,
        in_specs=placed,
        out_specs=(P("block", "tile", None, None), P("tile", None, None)),
        check_vma=False,
    )
```

```python
import jax
import jax.numpy as jnp
from jax import lax
from jax.experimental import pallas as pl
from jax.experimental.pallas import tpu as pltpu
from jax.sharding import PartitionSpec as P

GROUPS = 32
norm_eps = 1e-06


F32 = jnp.float32
BF16 = jnp.bfloat16
SPLIT = 16


class Sizes:
    def __init__(self, acts, weights, cotangent, tiles, blocks):
        self.frames, low_rows, self.cols, self.chans = acts.shape
        self.taps, self.outs = weights.shape[1:]
        self.tiles, self.blocks = tiles, blocks
        self.inner = 1 << (tiles.bit_length() // 2)
        self.outer = tiles // self.inner
        self.pairs = self.inner // 2
        self.per = self.chans // GROUPS
        self.gp = 16
        self.rb = self.outer * self.gp
        self.cells = self.frames * self.cols
        self.wide = 2 * self.cols
        self.grad_frames = self.frames * (2 if blocks > 1 else 1)
        self.first = max(0, 3 - self.frames * blocks)
        self.used = 9 * (3 - self.first)
        self.half = -(-self.used * self.per // 32) * 16
        self.sent = 2 * self.half
        self.wrows = self.sent + self.half
        self.lo = 128
        self.hi = self.outs - self.lo
        self.order = [*range(1, self.outer, 2), *range(0, self.outer, 2)]
        self.grows = 2 * self.grad_frames * self.outs
        self.count = float(low_rows * tiles * self.cols * self.per)
        if low_rows != 1 or tiles != GROUPS or self.hi != 64 or self.outer != 4:
            raise ValueError("unsupported sizes")


def swap(value, mask):
    count = lax.axis_size("tile")
    return lax.ppermute(value, "tile", [(i, i ^ mask) for i in range(count)])


def place(g):
    me = lax.axis_index("tile")
    return lax.div(me, g.inner), lax.rem(me, g.inner)


def iota(shape, dim):
    return lax.broadcasted_iota(jnp.int32, shape, dim)


def dot(a, b, dims=((1,), (0,))):
    return lax.dot_general(a, b, (dims, ((), ())), preferred_element_type=F32)


def channel_select(g, w, count):
    shape = (count * g.rb, g.chans)
    row = iota(shape, 0)
    block = row >> (g.rb.bit_length() - 1)
    group = (row & (g.rb - 1)) >> 4
    lane = row & (g.gp - 1)
    chan = g.per * (g.inner * group + (w ^ block)) + lane
    return (chan == iota(shape, 1)) & (lane < g.per)


def column_select(g):
    shape = (g.cells, g.frames * 3 * g.wide)
    row, col = iota(shape, 0), iota(shape, 1)
    bits = g.wide.bit_length() - 1
    part = col >> bits
    frame, shift = part, part
    frame = (part >= 3).astype(jnp.int32)
    for f in range(2, g.frames):
        frame = frame + (part >= 3 * f).astype(jnp.int32)
    shift = part - 3 * frame
    low = ((col & (g.wide - 1)) + shift - 1) >> 1
    inside = (low >= 0) & (low < g.cols)
    return (inside & (low + frame * g.cols == row)).astype(BF16)


def split(value, parts):
    out = []
    for _ in range(parts):
        piece = value.astype(BF16)
        out.append(piece)
        value = value - piece.astype(F32)
    return out


def sort_acts_kernel(g, acts_ref, *out_refs):
    _, w = place(g)
    pick = channel_select(g, w, g.inner).astype(BF16)
    blocks = dot(pick, acts_ref[...], ((1,), (1,))).astype(BF16)
    for k, ref in enumerate(out_refs):
        ref[...] = blocks[2 * k * g.rb : 2 * (k + 1) * g.rb].reshape(2, g.rb, g.cells)


def pack_rows(g, value):
    hi = jnp.concatenate([value[:, g.lo :], jnp.zeros((g.sent, 64), F32)], axis=1)
    lane = iota((g.half, 128), 1)
    both = jnp.where(lane < 64, hi[: g.half], pltpu.roll(hi[g.half :], 64, 1))
    return jnp.concatenate([value[:, : g.lo], both], axis=0).astype(BF16)


def unpack_rows(g, packed):
    both = packed[g.sent :].astype(F32)
    lane = iota(both.shape, 1)
    first = jnp.where(lane < 64, both, 0.0)
    second = jnp.where(lane < 64, pltpu.roll(both, 64, 1), 0.0)
    hi = jnp.concatenate([first, second], axis=0).astype(BF16)
    return jnp.concatenate([packed[: g.sent], hi], axis=1)


def pack_weights_kernel(g, weights_ref, out_ref):
    total = jnp.zeros((g.sent, g.outs), F32)
    row, tap = iota((g.sent, g.taps), 0), iota((g.sent, g.taps), 1) - 9 * g.first
    for i in range(g.per):
        pick = (row == tap * g.per + i) & (tap >= 0)
        total = total + dot(pick.astype(BF16), weights_ref[i])
    out_ref[...] = pack_rows(g, total)


def totals(g, first, second):
    pad = jnp.zeros((8 - g.outer, g.cells), F32)
    out = []
    for value in (first, second):
        out += [jnp.sum(value.reshape(g.outer, g.gp, g.cells), axis=1)]
        if g.outer < 8:
            out += [pad]
    return jnp.concatenate(out, axis=0)


def put_stats(ref, stats):
    for i, piece in enumerate(split(stats, 3)):
        ref[i * SPLIT : (i + 1) * SPLIT] = piece


def send_stats(g, ref, stats, z, rows_ref, parts):
    put_stats(ref, stats)
    last, even = rows_ref.shape[0] - 1, (z & 1) == 0
    for n, row in enumerate((jnp.where(even, last, 0), jnp.where(even, 0, last))):
        edge = rows_ref[row]
        for i, piece in enumerate(split(edge, parts) if parts > 1 else [edge.astype(BF16)]):
            at = 3 * SPLIT + (n * parts + i) * g.rb
            ref[at : at + g.rb] = piece


def step_kernel(g, stats_ref, received_ref, total_ref, send_ref):
    stats = add_stats(stats_ref[...], [received_ref])
    total_ref[...] = stats
    put_stats(send_ref, stats)
    count = send_ref.shape[0] - 3 * SPLIT
    send_ref[3 * SPLIT :] = received_ref[3 * SPLIT + count :]


def edges(g, z, received, parts):
    near, far = (
        sum(
            ref[3 * SPLIT + i * g.rb : 3 * SPLIT + (i + 1) * g.rb].astype(F32)
            for i in range(parts)
        )
        for ref in received
    )
    odd = (z & 1) == 1
    above = jnp.where(odd, near, jnp.where((z ^ 3) == z - 1, far, 0.0))
    below = jnp.where(odd, jnp.where((z ^ 3) == z + 1, far, 0.0), near)
    return above, below


def stats_kernel(g, *refs):
    direct, (crossed, rows_ref, stats_ref, send_ref) = refs[: g.pairs], refs[g.pairs :]
    z, w = place(g)
    first = jnp.zeros((g.rb, g.cells), F32)
    second = jnp.zeros((g.rb, g.cells), F32)
    for k in range(g.pairs):
        for j, block in enumerate((direct[k][0], crossed[k])):
            rows_ref[w ^ (2 * k + j)] = block
            wide = block.astype(F32)
            first = first + wide
            second = second + wide * wide
    stats = totals(g, first, second)
    stats_ref[...] = stats
    send_stats(g, send_ref, stats, z, rows_ref, 1)


def add_stats(own, received):
    for ref in received:
        for i in range(3):
            own = own + ref[i * SPLIT : (i + 1) * SPLIT].astype(F32)
    return own


def spread(g, stats):
    lane = iota((SPLIT, g.cells), 1)
    whole = jnp.zeros((SPLIT, g.cells), F32)
    for t in range(g.frames):
        mine = (lane >= t * g.cols) & (lane < (t + 1) * g.cols)
        part = jnp.sum(jnp.where(mine, stats, 0.0), axis=1, keepdims=True)
        whole = jnp.where(mine, part, whole)
    return tuple(
        jnp.concatenate(
            [
                jnp.broadcast_to(whole[s + q : s + q + 1], (g.gp, g.cells))
                for q in range(g.outer)
            ],
            axis=0,
        )
        for s in (0, 8)
    )


def prepare_weights_kernel(g, *refs):
    *packed, out_ref = refs
    z, _ = place(g)
    shape = (g.used * g.gp, g.sent)
    row, col = iota(shape, 0), iota(shape, 1)
    tap, lane = row >> 4, row & (g.gp - 1)
    pick = ((col == tap * g.per + lane) & (lane < g.per)).astype(BF16)
    blocks = [(ref, at) for ref in packed for at in range(0, ref.shape[0], g.wrows)]
    for k, (ref, at) in enumerate(blocks):
        value = dot(pick, unpack_rows(g, ref[at : at + g.wrows])).astype(BF16)
        out_ref[:, z ^ k] = value.reshape(g.used, g.gp, 256)


def meetings(g, later):
    pairs = [(a, later + a - 2) for a in range(g.first, 3)]
    return [(a, t) for a, t in pairs if 0 <= t < g.frames]


def fine_rows(g, ref, later):
    at = 2 * later * g.outs
    return jnp.concatenate([ref[at : at + g.outs], ref[at + g.outs : at + 2 * g.outs]], axis=1)


def lanes_of(g, t, e):
    return slice((3 * t + e) * g.wide, (3 * t + e + 1) * g.wide)


def field_kernel(g, j, *refs):
    *tiles, weights_ref, field = refs
    _, w = place(g)
    rb, wide = g.rb, g.wide
    field[...] = jnp.zeros_like(field)
    for k, ref in enumerate(tiles):
        row = w ^ (2 * k + j)
        for later in range(g.grad_frames):
            pairs = meetings(g, later)
            if not pairs:
                continue
            low, high = pairs[0][0] - g.first, pairs[-1][0] - g.first + 1
            taps = weights_ref[9 * low : 9 * high].reshape(9 * (high - low) * rb, 256)
            every = dot(taps[:, : g.outs], fine_rows(g, ref, later))
            for n, (_, t) in enumerate(pairs):
                back = every[9 * n * rb : 9 * (n + 1) * rb]
                part = lambda b, e, fine: back[
                    (3 * b + e) * rb : (3 * b + e + 1) * rb, fine * wide : (fine + 1) * wide
                ]
                for e in range(3):
                    lanes = lanes_of(g, t, e)
                    field[row, :, lanes] += part(0, e, 0)
                    field[row + 1, :, lanes] += (part(1, e, 0) + part(2, e, 0)) + (
                        part(0, e, 1) + part(1, e, 1)
                    )
                    field[row + 2, :, lanes] += part(2, e, 1)


def norm_grad_kernel(g, *refs):
    rows_ref, stats_ref, gamma_ref, beta_ref, field_ref, other_ref, *refs = refs
    received, refs = refs[:2], refs[2:]
    normed_ref, hidden_ref, inv_ref, sums_ref, grad_ref, send_ref, slope_ref, hidden_scratch = refs
    z, w = place(g)
    rb = g.rb
    total, total_sq = spread(g, add_stats(stats_ref[...], received[1:]))
    mean = total / g.count
    inv = lax.rsqrt(total_sq / g.count - mean * mean + norm_eps)
    inv_ref[...] = inv
    pick = channel_select(g, w, 1)
    gamma = jnp.sum(jnp.where(pick, gamma_ref[...].reshape(1, g.chans), 0.0), axis=1, keepdims=True)
    beta = jnp.sum(jnp.where(pick, beta_ref[...].reshape(1, g.chans), 0.0), axis=1, keepdims=True)

    def activate(place_at, block, present):
        normed = (block.astype(F32) - mean) * inv
        shifted = normed * gamma + beta
        gate = jax.nn.sigmoid(shifted)
        normed_ref[place_at] = normed
        hidden = (shifted * gate * present).astype(BF16).reshape(g.outer, g.gp, g.cells)
        hidden_scratch[...] = hidden
        for at, k in enumerate(g.order):
            hidden_ref[at, place_at] = hidden_scratch[z ^ k]
        slope_ref[place_at] = gate * (1.0 + shifted * (1.0 - gate)) * gamma * present

    above, below = edges(g, z, received, 1)
    activate(0, above, jnp.where(z > 0, 1.0, 0.0))
    activate(g.inner + 1, below, jnp.where(z < g.outer - 1, 1.0, 0.0))

    @pl.loop(0, g.inner)
    def _(i):
        activate(i + 1, rows_ref[i], 1.0)

    count = g.inner + 2
    select = column_select(g)
    flat = (field_ref[...] + other_ref[...]).reshape(count * rb, g.frames * 3 * g.wide)
    pieces = split(flat, 2)
    act_grad = dot(pieces[0], select, ((1,), (1,))) + dot(pieces[1], select, ((1,), (1,)))
    grad = act_grad.reshape(count, rb, g.cells) * slope_ref[...]
    grad_ref[...] = grad
    sums = totals(g, jnp.sum(grad, axis=0), jnp.sum(grad * normed_ref[...], axis=0))
    sums_ref[...] = sums
    send_stats(g, send_ref, sums, z, grad_ref, 1)


def kernel_terms(g, first, direct, crossed, hidden_ref, acc, ups):
    _, w = place(g)
    part = acc.shape[0]
    flat = hidden_ref[first : first + part].reshape(-1, g.cells)
    ups[...] = dot(flat, column_select(g)).astype(BF16).reshape(ups.shape)
    started = set()
    for later in range(g.grad_frames):
        for a, t in meetings(g, later):
            left, right = [], []
            for k in range(g.pairs):
                for j, ref in enumerate((direct[k], crossed[k])):
                    row = w ^ (2 * k + j)
                    pieces = []
                    for group in range(part):
                        for upper, lower in ((0, 1), (1, 1), (1, 2)):
                            for e in range(3):
                                lanes = lanes_of(g, t, e)
                                sides = [ups[group, row + at, :, lanes] for at in (upper, lower)]
                                pieces.append(jnp.concatenate(sides, axis=1))
                    left.append(jnp.concatenate(pieces, axis=0))
                    right.append(fine_rows(g, ref, later))
            terms = dot(
                jnp.concatenate(left, axis=1), jnp.concatenate(right, axis=1), ((1,), (1,))
            ).reshape(part, 9, g.gp, g.outs)
            taps = slice(9 * (a - g.first), 9 * (a - g.first + 1))
            if a in started:
                acc[:, taps] += terms
            else:
                acc[:, taps] = terms
                started.add(a)


def sent_order(g):
    shape = (g.sent, g.used * g.gp)
    row, col = iota(shape, 0), iota(shape, 1)
    tap, lane = col >> 4, col & (g.gp - 1)
    return ((row == tap * g.per + lane) & (lane < g.per)).astype(BF16)


def sent_terms_kernel(g, *refs):
    direct, crossed, refs = refs[: g.pairs], refs[g.pairs : 2 * g.pairs], refs[2 * g.pairs :]
    hidden_ref, send_ref, acc, ups = refs
    kernel_terms(g, 0, direct, crossed, hidden_ref, acc, ups)
    pick = sent_order(g)
    for i in range(g.outer // 2):
        terms = acc[i].reshape(g.used * g.gp, g.outs).astype(BF16)
        send_ref[i * g.wrows : (i + 1) * g.wrows] = pack_rows(g, dot(pick, terms))


def kept_terms_kernel(g, *refs):
    direct, crossed, refs = refs[: g.pairs], refs[g.pairs : 2 * g.pairs], refs[2 * g.pairs :]
    hidden_ref, own_ref, *kept, acc, ups = refs
    kernel_terms(g, g.outer // 2, direct, crossed, hidden_ref, acc, ups)
    own_ref[...] = acc[0].reshape(g.used * g.gp, g.outs)
    pick = sent_order(g)
    for i in range(1, g.outer // 2):
        terms = acc[i].reshape(g.used * g.gp, g.outs)
        kept[0][i - 1] = sum(dot(pick, piece) for piece in split(terms, 2))


def halve_kernel(g, bit, keep_ref, received_ref, *refs):
    send_ref, *kept = refs
    for i in range(keep_ref.shape[0]):
        block = received_ref[(i + 1) * g.wrows : (i + 2) * g.wrows]
        total = keep_ref[i] + unpack_rows(g, block).astype(F32)[:, : g.outs]
        if i % 2:
            kept[0][i // 2] = total
        else:
            send_ref[i // 2 * g.wrows : (i // 2 + 1) * g.wrows] = pack_rows(g, total)


def finish_kernel(g, *refs):
    sums_ref, grad_ref, normed_ref, inv_ref, *refs = refs
    received, sends = refs[:2], refs[2:]
    z, w = place(g)
    first, second = spread(g, add_stats(sums_ref[...], received[1:]))
    first, second = first / g.count, second / g.count
    inv = inv_ref[...]
    above, below = edges(g, z, received, 1)
    for k, ref in enumerate(sends):
        for j in range(2):
            row = w ^ (2 * k + j)
            grad = grad_ref[row + 1]
            grad = grad + jnp.where(row == 0, above, 0.0)
            grad = grad + jnp.where(row == g.inner - 1, below, 0.0)
            ref[j] = (inv * (grad - first - normed_ref[row + 1] * second)).astype(BF16)


def unpack_kernel(g, own_ref, *refs):
    steps = g.outer.bit_length() - 1
    received, refs = refs[:steps], refs[steps:]
    direct, (crossed, acts_ref, out_ref, low, high) = refs[: g.pairs], refs[g.pairs :]
    _, w = place(g)
    pick = channel_select(g, w, g.inner).astype(BF16)
    blocks = []
    for k in range(g.pairs):
        blocks += [direct[k][0], crossed[k]]
    d_acts = dot(jnp.concatenate(blocks, axis=0), pick, ((0,), (0,)))
    acts_ref[...] = d_acts.astype(BF16).reshape(acts_ref.shape)

    step = 32
    shape = (g.per * step, g.sent)
    row, col = iota(shape, 0), iota(shape, 1)
    tap, lane = row & (step - 1), row >> 5
    pick = ((col == tap * g.per + lane) & (tap < g.used)).astype(BF16)
    total = jnp.zeros((g.per * step, 256), F32)
    for ref in received:
        total = total + dot(pick, unpack_rows(g, ref[: g.wrows]))
    low[...] = own_ref[:, : g.lo]
    high[:, : g.hi] = own_ref[:, g.lo :]
    for i in range(g.per):
        at = pl.ds(i, g.used, stride=g.gp)
        there = total[i * step : i * step + g.used]
        if g.first:
            out_ref[i, : 9 * g.first, :] = jnp.zeros((9 * g.first, g.outs), F32)
        out_ref[i, 9 * g.first :, : g.lo] = low[at, :] + there[:, : g.lo]
        out_ref[i, 9 * g.first :, g.lo :] = high[at, :][:, : g.hi] + there[:, g.lo : g.outs]


def call(g, kernel, name, outs, args, scratch=(), flops=0, after=()):
    shapes = [jax.ShapeDtypeStruct(shape, kind) for shape, kind in outs]
    whole = pl.BlockSpec(memory_space=pltpu.VMEM)
    moved = sum(a.size * a.dtype.itemsize for a in list(args) + shapes)
    count = len(args)
    rest = count + len(after)
    return pl.pallas_call(
        lambda *refs: kernel(g, *refs[:count], *refs[rest:]),
        out_shape=shapes,
        in_specs=[whole] * count + [pl.BlockSpec(memory_space=pl.ANY)] * len(after),
        out_specs=[whole] * len(shapes),
        scratch_shapes=list(scratch),
        compiler_params=pltpu.CompilerParams(vmem_limit_bytes=48 * 1024 * 1024),
        cost_estimate=pl.CostEstimate(flops=flops, bytes_accessed=moved, transcendentals=0),
        name=name,
    )(*args, *after)


def copy_kernel(g, in_ref, out_ref):
    out_ref[...] = in_ref[...]


def join_kernel(g, *refs):
    *parts, out_ref = refs
    at = 0
    for ref in parts:
        out_ref[at : at + ref.shape[0]] = ref[...]
        at += ref.shape[0]


def pass_on(g, value, after):
    return call(g, copy_kernel, "pass_on", [(value.shape, value.dtype)], [value], after=after)[0]


def cross_kernel(g, *refs):
    *blocks, out_ref = refs
    for k, ref in enumerate(blocks):
        out_ref[k] = ref[1]


def cross(g, name, direct):
    shape = (g.pairs, g.rb, g.cells)
    (out,) = call(g, cross_kernel, name, [(shape, BF16)], direct)
    return swap(out, 1)


def shards(acts, gamma, beta, weights, cotangent):
    g = Sizes(acts, weights, cotangent, lax.axis_size("tile"), lax.axis_size("block"))
    if g.blocks > 1:
        pairs = [(i + 1, i) for i in range(g.blocks - 1)]
        following = lax.ppermute(cotangent, "block", pairs)
        cotangent = jnp.concatenate([cotangent, following], 0)
    count = g.inner + 2
    block = ((2, g.rb, g.cells), BF16)
    rows_shape = ((count, g.rb, g.cells), F32)
    stats_shape = ((SPLIT, g.cells), F32)
    packed_shape = ((g.wrows, 128), BF16)
    wide_shape = (count, g.rb, g.frames * 3 * g.wide)
    sums_shape = lambda edges: ((3 * SPLIT + edges * g.rb, 128), BF16)

    def over_z(name, stats, send, parts, after):
        near = swap(send, g.inner)
        outs = [stats_shape, sums_shape(parts)]
        total, send = call(g, step_kernel, name, outs, [stats, near], after=after)
        return total, send, [near, swap(send, 2 * g.inner)]

    packed = list(
        call(g, pack_weights_kernel, "pack_weights", [packed_shape], [weights], flops=6 * 10**9)
    )
    for bit in range(g.outer.bit_length() - 1):
        whole = packed[0]
        if bit:
            shape = ((g.wrows << bit, 128), BF16)
            (whole,) = call(g, join_kernel, "join_kernel_rows", [shape], packed)
        packed.append(swap(whole, g.inner << bit))
    sends = call(
        g,
        sort_acts_kernel,
        "sort_acts",
        [block] * g.pairs,
        [acts.reshape(g.cells, g.chans)],
        flops=2*10**9,
    )
    blocks = [sends[0]] + [swap(sends[k], 2 * k) for k in range(1, g.pairs)]
    blocks.append(cross(g, "cross_acts", blocks))
    turned = jnp.swapaxes(cotangent, 2, 3).reshape(g.grows, g.wide)
    direct = [turned] + [swap(turned, 2 * k) for k in range(1, g.pairs)]
    arrived = direct + [swap(v, 1) for v in direct]

    rows, stats, send = call(
        g,
        stats_kernel,
        "stats",
        [((g.inner, g.rb, g.cells), BF16), stats_shape, sums_shape(2)],
        blocks,
        flops=5*10**9,
    )
    kernel_shape = ((g.used, g.outer, g.gp, 256), BF16)
    (rows_of_kernel,) = call(g, prepare_weights_kernel, "kernel_rows", [kernel_shape], packed, flops=7*10**9)
    flops = 2 * 2 * g.inner * 9 * g.rb * 256 * 256 * g.grad_frames
    fields = [
        call(
            g,
            lambda g, *refs, j=j: field_kernel(g, j, *refs),
            "field_grad",
            [(wide_shape, F32)],
            arrived[j * g.pairs : (j + 1) * g.pairs] + [rows_of_kernel],
            flops=flops // 2,
        )[0]
        for j in range(2)
    ]
    stats, _, received = over_z("add_stats", stats, send, 1, ())
    hidden_shape = ((g.outer, count, g.gp, g.cells), BF16)
    normed, hidden, inv, sums, grad, send = call(
        g,
        norm_grad_kernel,
        "norm_grad",
        [rows_shape, hidden_shape, ((g.rb, g.cells), F32), stats_shape, rows_shape, sums_shape(2)],
        [rows, stats, gamma, beta] + fields + received,
        [pltpu.VMEM(*rows_shape), pltpu.VMEM((g.outer, g.gp, g.cells), BF16)],
    )
    half = g.outer // 2
    kept_shape = lambda count: [((count, g.sent, g.outs), F32)] if count else []
    scratch = [
        pltpu.VMEM((half, g.used, g.gp, g.outs), F32),
        pltpu.VMEM((half, count, g.gp, wide_shape[-1]), BF16),
    ]
    (terms,) = call(
        g,
        sent_terms_kernel,
        "sent_terms",
        [((half * g.wrows, 128), BF16)],
        arrived + [hidden],
        scratch,
        flops // 2,
    )
    sums, send, received = over_z("add_sums", sums, send, 1, [terms])
    terms = [swap(pass_on(g, terms, [send]), g.inner)]
    own, *kept = call(
        g,
        kept_terms_kernel,
        "kept_terms",
        [((g.used * g.gp, g.outs), F32)] + kept_shape(half - 1),
        arrived + [hidden],
        scratch,
        flops // 2,
        after=[send],
    )
    sends = call(
        g,
        finish_kernel,
        "finish",
        [block] * g.pairs,
        [sums, grad, normed, inv] + received,
        after=[own],
    )
    direct = [sends[0]] + [swap(sends[k], 2 * k) for k in range(1, g.pairs)]
    bit = 1
    while kept:
        half //= 2
        send, *kept = call(
            g,
            lambda g, *refs, bit=bit: halve_kernel(g, bit, *refs),
            "halve",
            [((half * g.wrows, 128), BF16)] + kept_shape(half - 1),
            [kept[0], terms[-1]],
        )
        terms.append(swap(send, g.inner << bit))
        bit += 1
    crossed = cross(g, "cross_grads", direct)
    d_acts, d_weights = call(
        g,
        unpack_kernel,
        "unpack",
        [(acts.shape, BF16), (weights.shape, F32)],
        [own] + terms + direct + [crossed],
        [pltpu.VMEM((g.used * g.gp, 128), F32)] * 2,
    )
    if g.blocks > 1:
        d_weights = lax.psum(d_weights, "block")
    return (d_acts, d_weights)


def solution(mesh):
    placed = (
        P("block", "tile", None, None),
        P(),
        P(),
        P("tile", None, None),
        P("block", "tile", None, None),
    )
    return jax.shard_map(
        shards,
        mesh=mesh,
        in_specs=placed,
        out_specs=(P("block", "tile", None, None), P("tile", None, None)),
        check_vma=False,
    )
```

```python
import jax
import jax.numpy as jnp
from jax import lax
from jax.experimental import pallas as pl
from jax.experimental.pallas import tpu as pltpu
from jax.sharding import PartitionSpec as P

GROUPS = 32
norm_eps = 1e-06


F32 = jnp.float32
BF16 = jnp.bfloat16
SPLIT = 16


class Sizes:
    def __init__(self, acts, weights, cotangent, tiles, blocks):
        self.frames, low_rows, self.cols, self.chans = acts.shape
        self.taps, self.outs = weights.shape[1:]
        self.tiles, self.blocks = tiles, blocks
        self.inner = 1 << (tiles.bit_length() // 2)
        self.outer = tiles // self.inner
        self.pairs = self.inner // 2
        self.per = self.chans // GROUPS
        self.gp = 16
        self.rb = self.outer * self.gp
        self.cells = self.frames * self.cols
        self.wide = 2 * self.cols
        self.grad_frames = self.frames * (2 if blocks > 1 else 1)
        self.first = max(0, 3 - self.frames * blocks)
        self.used = 9 * (3 - self.first)
        self.half = -(-self.used * self.per // 32) * 16
        self.sent = 2 * self.half
        self.wrows = self.sent + self.half
        self.lo = 128
        self.hi = self.outs - self.lo
        self.order = [*range(1, self.outer, 2), *range(0, self.outer, 2)]
        self.grows = 2 * self.grad_frames * self.outs
        self.count = float(low_rows * tiles * self.cols * self.per)
        if low_rows != 1 or tiles != GROUPS or self.hi != 64 or self.outer != 4:
            raise ValueError("unsupported sizes")


def swap(value, mask):
    count = lax.axis_size("tile")
    return lax.ppermute(value, "tile", [(i, i ^ mask) for i in range(count)])


def place(g):
    me = lax.axis_index("tile")
    return lax.div(me, g.inner), lax.rem(me, g.inner)


def iota(shape, dim):
    return lax.broadcasted_iota(jnp.int32, shape, dim)


def dot(a, b, dims=((1,), (0,))):
    return lax.dot_general(a, b, (dims, ((), ())), preferred_element_type=F32)


def channel_select(g, w, count):
    shape = (count * g.rb, g.chans)
    row = iota(shape, 0)
    block = row >> (g.rb.bit_length() - 1)
    group = (row & (g.rb - 1)) >> 4
    lane = row & (g.gp - 1)
    chan = g.per * (g.inner * group + (w ^ block)) + lane
    return (chan == iota(shape, 1)) & (lane < g.per)


def column_select(g):
    shape = (g.cells, g.frames * 3 * g.wide)
    row, col = iota(shape, 0), iota(shape, 1)
    bits = g.wide.bit_length() - 1
    part = col >> bits
    frame, shift = part, part
    frame = (part >= 3).astype(jnp.int32)
    for f in range(2, g.frames):
        frame = frame + (part >= 3 * f).astype(jnp.int32)
    shift = part - 3 * frame
    low = ((col & (g.wide - 1)) + shift - 1) >> 1
    inside = (low >= 0) & (low < g.cols)
    return (inside & (low + frame * g.cols == row)).astype(BF16)


def split(value, parts):
    out = []
    for _ in range(parts):
        piece = value.astype(BF16)
        out.append(piece)
        value = value - piece.astype(F32)
    return out


def sort_acts_kernel(g, acts_ref, *out_refs):
    _, w = place(g)
    pick = channel_select(g, w, g.inner).astype(BF16)
    blocks = dot(pick, acts_ref[...], ((1,), (1,))).astype(BF16)
    for k, ref in enumerate(out_refs):
        ref[...] = blocks[2 * k * g.rb : 2 * (k + 1) * g.rb].reshape(2, g.rb, g.cells)


def pack_rows(g, value):
    hi = jnp.concatenate([value[:, g.lo :], jnp.zeros((g.sent, 64), F32)], axis=1)
    lane = iota((g.half, 128), 1)
    both = jnp.where(lane < 64, hi[: g.half], pltpu.roll(hi[g.half :], 64, 1))
    return jnp.concatenate([value[:, : g.lo], both], axis=0).astype(BF16)


def unpack_rows(g, packed):
    both = packed[g.sent :].astype(F32)
    lane = iota(both.shape, 1)
    first = jnp.where(lane < 64, both, 0.0)
    second = jnp.where(lane < 64, pltpu.roll(both, 64, 1), 0.0)
    hi = jnp.concatenate([first, second], axis=0).astype(BF16)
    return jnp.concatenate([packed[: g.sent], hi], axis=1)


def pack_weights_kernel(g, weights_ref, out_ref):
    total = jnp.zeros((g.sent, g.outs), F32)
    row, tap = iota((g.sent, g.taps), 0), iota((g.sent, g.taps), 1) - 9 * g.first
    for i in range(g.per):
        pick = (row == tap * g.per + i) & (tap >= 0)
        total = total + dot(pick.astype(BF16), weights_ref[i])
    out_ref[...] = pack_rows(g, total)


def totals(g, first, second):
    pad = jnp.zeros((8 - g.outer, g.cells), F32)
    out = []
    for value in (first, second):
        out += [jnp.sum(value.reshape(g.outer, g.gp, g.cells), axis=1)]
        if g.outer < 8:
            out += [pad]
    return jnp.concatenate(out, axis=0)


def put_stats(ref, stats):
    for i, piece in enumerate(split(stats, 3)):
        ref[i * SPLIT : (i + 1) * SPLIT] = piece


def send_stats(g, ref, stats, z, rows_ref, parts):
    put_stats(ref, stats)
    last, even = rows_ref.shape[0] - 1, (z & 1) == 0
    for n, row in enumerate((jnp.where(even, last, 0), jnp.where(even, 0, last))):
        edge = rows_ref[row]
        for i, piece in enumerate(split(edge, parts) if parts > 1 else [edge.astype(BF16)]):
            at = 3 * SPLIT + (n * parts + i) * g.rb
            ref[at : at + g.rb] = piece


def step_kernel(g, stats_ref, received_ref, total_ref, send_ref):
    stats = add_stats(stats_ref[...], [received_ref])
    total_ref[...] = stats
    put_stats(send_ref, stats)
    count = send_ref.shape[0] - 3 * SPLIT
    send_ref[3 * SPLIT :] = received_ref[3 * SPLIT + count :]


def edges(g, z, received, parts):
    near, far = (
        sum(
            ref[3 * SPLIT + i * g.rb : 3 * SPLIT + (i + 1) * g.rb].astype(F32)
            for i in range(parts)
        )
        for ref in received
    )
    odd = (z & 1) == 1
    above = jnp.where(odd, near, jnp.where((z ^ 3) == z - 1, far, 0.0))
    below = jnp.where(odd, jnp.where((z ^ 3) == z + 1, far, 0.0), near)
    return above, below


def stats_kernel(g, *refs):
    direct, (crossed, rows_ref, stats_ref, send_ref) = refs[: g.pairs], refs[g.pairs :]
    z, w = place(g)
    first = jnp.zeros((g.rb, g.cells), F32)
    second = jnp.zeros((g.rb, g.cells), F32)
    for k in range(g.pairs):
        for j, block in enumerate((direct[k][0], crossed[k])):
            rows_ref[w ^ (2 * k + j)] = block
            wide = block.astype(F32)
            first = first + wide
            second = second + wide * wide
    stats = totals(g, first, second)
    stats_ref[...] = stats
    send_stats(g, send_ref, stats, z, rows_ref, 1)


def add_stats(own, received):
    for ref in received:
        for i in range(3):
            own = own + ref[i * SPLIT : (i + 1) * SPLIT].astype(F32)
    return own


def spread(g, stats):
    lane = iota((SPLIT, g.cells), 1)
    whole = jnp.zeros((SPLIT, g.cells), F32)
    for t in range(g.frames):
        mine = (lane >= t * g.cols) & (lane < (t + 1) * g.cols)
        part = jnp.sum(jnp.where(mine, stats, 0.0), axis=1, keepdims=True)
        whole = jnp.where(mine, part, whole)
    return tuple(
        jnp.concatenate(
            [
                jnp.broadcast_to(whole[s + q : s + q + 1], (g.gp, g.cells))
                for q in range(g.outer)
            ],
            axis=0,
        )
        for s in (0, 8)
    )


def prepare_weights_kernel(g, *refs):
    *packed, out_ref = refs
    z, _ = place(g)
    shape = (g.used * g.gp, g.sent)
    row, col = iota(shape, 0), iota(shape, 1)
    tap, lane = row >> 4, row & (g.gp - 1)
    pick = ((col == tap * g.per + lane) & (lane < g.per)).astype(BF16)
    blocks = [(ref, at) for ref in packed for at in range(0, ref.shape[0], g.wrows)]
    for k, (ref, at) in enumerate(blocks):
        value = dot(pick, unpack_rows(g, ref[at : at + g.wrows])).astype(BF16)
        out_ref[:, z ^ k] = value.reshape(g.used, g.gp, 256)


def meetings(g, later):
    pairs = [(a, later + a - 2) for a in range(g.first, 3)]
    return [(a, t) for a, t in pairs if 0 <= t < g.frames]


def fine_rows(g, ref, later):
    at = 2 * later * g.outs
    return jnp.concatenate([ref[at : at + g.outs], ref[at + g.outs : at + 2 * g.outs]], axis=1)


def lanes_of(g, t, e):
    return slice((3 * t + e) * g.wide, (3 * t + e + 1) * g.wide)


def field_kernel(g, j, *refs):
    *tiles, weights_ref, field = refs
    _, w = place(g)
    rb, wide = g.rb, g.wide
    field[...] = jnp.zeros_like(field)
    for k, ref in enumerate(tiles):
        row = w ^ (2 * k + j)
        for later in range(g.grad_frames):
            pairs = meetings(g, later)
            if not pairs:
                continue
            low, high = pairs[0][0] - g.first, pairs[-1][0] - g.first + 1
            taps = weights_ref[9 * low : 9 * high].reshape(9 * (high - low) * rb, 256)
            every = dot(taps[:, : g.outs], fine_rows(g, ref, later))
            for n, (_, t) in enumerate(pairs):
                back = every[9 * n * rb : 9 * (n + 1) * rb]
                part = lambda b, e, fine: back[
                    (3 * b + e) * rb : (3 * b + e + 1) * rb, fine * wide : (fine + 1) * wide
                ]
                for e in range(3):
                    lanes = lanes_of(g, t, e)
                    field[row, :, lanes] += part(0, e, 0)
                    field[row + 1, :, lanes] += (part(1, e, 0) + part(2, e, 0)) + (
                        part(0, e, 1) + part(1, e, 1)
                    )
                    field[row + 2, :, lanes] += part(2, e, 1)


def norm_grad_kernel(g, *refs):
    rows_ref, stats_ref, gamma_ref, beta_ref, field_ref, other_ref, *refs = refs
    received, refs = refs[:2], refs[2:]
    normed_ref, hidden_ref, inv_ref, sums_ref, grad_ref, send_ref, slope_ref, hidden_scratch = refs
    z, w = place(g)
    rb = g.rb
    total, total_sq = spread(g, add_stats(stats_ref[...], received[1:]))
    mean = total / g.count
    inv = lax.rsqrt(total_sq / g.count - mean * mean + norm_eps)
    inv_ref[...] = inv
    pick = channel_select(g, w, 1)
    gamma = jnp.sum(jnp.where(pick, gamma_ref[...].reshape(1, g.chans), 0.0), axis=1, keepdims=True)
    beta = jnp.sum(jnp.where(pick, beta_ref[...].reshape(1, g.chans), 0.0), axis=1, keepdims=True)

    def activate(place_at, block, present):
        normed = (block.astype(F32) - mean) * inv
        shifted = normed * gamma + beta
        gate = jax.nn.sigmoid(shifted)
        normed_ref[place_at] = normed
        hidden = (shifted * gate * present).astype(BF16).reshape(g.outer, g.gp, g.cells)
        hidden_scratch[...] = hidden
        for at, k in enumerate(g.order):
            hidden_ref[at, place_at] = hidden_scratch[z ^ k]
        slope_ref[place_at] = gate * (1.0 + shifted * (1.0 - gate)) * gamma * present

    above, below = edges(g, z, received, 1)
    activate(0, above, jnp.where(z > 0, 1.0, 0.0))
    activate(g.inner + 1, below, jnp.where(z < g.outer - 1, 1.0, 0.0))

    @pl.loop(0, g.inner)
    def _(i):
        activate(i + 1, rows_ref[i], 1.0)

    count = g.inner + 2
    select = column_select(g)
    flat = (field_ref[...] + other_ref[...]).reshape(count * rb, g.frames * 3 * g.wide)
    pieces = split(flat, 2)
    act_grad = dot(pieces[0], select, ((1,), (1,))) + dot(pieces[1], select, ((1,), (1,)))
    grad = act_grad.reshape(count, rb, g.cells) * slope_ref[...]
    grad_ref[...] = grad
    sums = totals(g, jnp.sum(grad, axis=0), jnp.sum(grad * normed_ref[...], axis=0))
    sums_ref[...] = sums
    send_stats(g, send_ref, sums, z, grad_ref, 2)


def kernel_terms(g, first, direct, crossed, hidden_ref, acc, ups):
    _, w = place(g)
    part = acc.shape[0]
    flat = hidden_ref[first : first + part].reshape(-1, g.cells)
    ups[...] = dot(flat, column_select(g)).astype(BF16).reshape(ups.shape)
    started = set()
    for later in range(g.grad_frames):
        for a, t in meetings(g, later):
            left, right = [], []
            for k in range(g.pairs):
                for j, ref in enumerate((direct[k], crossed[k])):
                    row = w ^ (2 * k + j)
                    pieces = []
                    for group in range(part):
                        for upper, lower in ((0, 1), (1, 1), (1, 2)):
                            for e in range(3):
                                lanes = lanes_of(g, t, e)
                                sides = [ups[group, row + at, :, lanes] for at in (upper, lower)]
                                pieces.append(jnp.concatenate(sides, axis=1))
                    left.append(jnp.concatenate(pieces, axis=0))
                    right.append(fine_rows(g, ref, later))
            terms = dot(
                jnp.concatenate(left, axis=1), jnp.concatenate(right, axis=1), ((1,), (1,))
            ).reshape(part, 9, g.gp, g.outs)
            taps = slice(9 * (a - g.first), 9 * (a - g.first + 1))
            if a in started:
                acc[:, taps] += terms
            else:
                acc[:, taps] = terms
                started.add(a)


def sent_order(g):
    shape = (g.sent, g.used * g.gp)
    row, col = iota(shape, 0), iota(shape, 1)
    tap, lane = col >> 4, col & (g.gp - 1)
    return ((row == tap * g.per + lane) & (lane < g.per)).astype(BF16)


def sent_terms_kernel(g, *refs):
    direct, crossed, refs = refs[: g.pairs], refs[g.pairs : 2 * g.pairs], refs[2 * g.pairs :]
    hidden_ref, send_ref, acc, ups = refs
    kernel_terms(g, 0, direct, crossed, hidden_ref, acc, ups)
    pick = sent_order(g)
    for i in range(g.outer // 2):
        terms = acc[i].reshape(g.used * g.gp, g.outs).astype(BF16)
        send_ref[i * g.wrows : (i + 1) * g.wrows] = pack_rows(g, dot(pick, terms))


def kept_terms_kernel(g, *refs):
    direct, crossed, refs = refs[: g.pairs], refs[g.pairs : 2 * g.pairs], refs[2 * g.pairs :]
    hidden_ref, own_ref, *kept, acc, ups = refs
    kernel_terms(g, g.outer // 2, direct, crossed, hidden_ref, acc, ups)
    own_ref[...] = acc[0].reshape(g.used * g.gp, g.outs)
    pick = sent_order(g)
    for i in range(1, g.outer // 2):
        terms = acc[i].reshape(g.used * g.gp, g.outs)
        kept[0][i - 1] = sum(dot(pick, piece) for piece in split(terms, 2))


def halve_kernel(g, bit, keep_ref, received_ref, *refs):
    send_ref, *kept = refs
    for i in range(keep_ref.shape[0]):
        block = received_ref[(i + 1) * g.wrows : (i + 2) * g.wrows]
        total = keep_ref[i] + unpack_rows(g, block).astype(F32)[:, : g.outs]
        if i % 2:
            kept[0][i // 2] = total
        else:
            send_ref[i // 2 * g.wrows : (i // 2 + 1) * g.wrows] = pack_rows(g, total)


def finish_kernel(g, *refs):
    sums_ref, grad_ref, normed_ref, inv_ref, *refs = refs
    received, sends = refs[:2], refs[2:]
    z, w = place(g)
    first, second = spread(g, add_stats(sums_ref[...], received[1:]))
    first, second = first / g.count, second / g.count
    inv = inv_ref[...]
    above, below = edges(g, z, received, 2)
    for k, ref in enumerate(sends):
        for j in range(2):
            row = w ^ (2 * k + j)
            grad = grad_ref[row + 1]
            grad = grad + jnp.where(row == 0, above, 0.0)
            grad = grad + jnp.where(row == g.inner - 1, below, 0.0)
            ref[j] = (inv * (grad - first - normed_ref[row + 1] * second)).astype(BF16)


def unpack_kernel(g, own_ref, *refs):
    steps = g.outer.bit_length() - 1
    received, refs = refs[:steps], refs[steps:]
    direct, (crossed, acts_ref, out_ref, low, high) = refs[: g.pairs], refs[g.pairs :]
    _, w = place(g)
    pick = channel_select(g, w, g.inner).astype(BF16)
    blocks = []
    for k in range(g.pairs):
        blocks += [direct[k][0], crossed[k]]
    d_acts = dot(jnp.concatenate(blocks, axis=0), pick, ((0,), (0,)))
    acts_ref[...] = d_acts.astype(BF16).reshape(acts_ref.shape)

    step = 32
    shape = (g.per * step, g.sent)
    row, col = iota(shape, 0), iota(shape, 1)
    tap, lane = row & (step - 1), row >> 5
    pick = ((col == tap * g.per + lane) & (tap < g.used)).astype(BF16)
    total = jnp.zeros((g.per * step, 256), F32)
    for ref in received:
        total = total + dot(pick, unpack_rows(g, ref[: g.wrows]))
    low[...] = own_ref[:, : g.lo]
    high[:, : g.hi] = own_ref[:, g.lo :]
    for i in range(g.per):
        at = pl.ds(i, g.used, stride=g.gp)
        there = total[i * step : i * step + g.used]
        if g.first:
            out_ref[i, : 9 * g.first, :] = jnp.zeros((9 * g.first, g.outs), F32)
        out_ref[i, 9 * g.first :, : g.lo] = low[at, :] + there[:, : g.lo]
        out_ref[i, 9 * g.first :, g.lo :] = high[at, :][:, : g.hi] + there[:, g.lo : g.outs]


def call(g, kernel, name, outs, args, scratch=(), flops=0, after=()):
    shapes = [jax.ShapeDtypeStruct(shape, kind) for shape, kind in outs]
    whole = pl.BlockSpec(memory_space=pltpu.VMEM)
    moved = sum(a.size * a.dtype.itemsize for a in list(args) + shapes)
    count = len(args)
    rest = count + len(after)
    return pl.pallas_call(
        lambda *refs: kernel(g, *refs[:count], *refs[rest:]),
        out_shape=shapes,
        in_specs=[whole] * count + [pl.BlockSpec(memory_space=pl.ANY)] * len(after),
        out_specs=[whole] * len(shapes),
        scratch_shapes=list(scratch),
        compiler_params=pltpu.CompilerParams(vmem_limit_bytes=48 * 1024 * 1024),
        cost_estimate=pl.CostEstimate(flops=flops, bytes_accessed=moved, transcendentals=0),
        name=name,
    )(*args, *after)


def copy_kernel(g, in_ref, out_ref):
    out_ref[...] = in_ref[...]


def join_kernel(g, *refs):
    *parts, out_ref = refs
    at = 0
    for ref in parts:
        out_ref[at : at + ref.shape[0]] = ref[...]
        at += ref.shape[0]


def pass_on(g, value, after):
    return call(g, copy_kernel, "pass_on", [(value.shape, value.dtype)], [value], after=after)[0]


def cross_kernel(g, *refs):
    *blocks, out_ref = refs
    for k, ref in enumerate(blocks):
        out_ref[k] = ref[1]


def cross(g, name, direct):
    shape = (g.pairs, g.rb, g.cells)
    (out,) = call(g, cross_kernel, name, [(shape, BF16)], direct)
    return swap(out, 1)


def shards(acts, gamma, beta, weights, cotangent):
    g = Sizes(acts, weights, cotangent, lax.axis_size("tile"), lax.axis_size("block"))
    if g.blocks > 1:
        pairs = [(i + 1, i) for i in range(g.blocks - 1)]
        following = lax.ppermute(cotangent, "block", pairs)
        cotangent = jnp.concatenate([cotangent, following], 0)
    count = g.inner + 2
    block = ((2, g.rb, g.cells), BF16)
    rows_shape = ((count, g.rb, g.cells), F32)
    stats_shape = ((SPLIT, g.cells), F32)
    packed_shape = ((g.wrows, 128), BF16)
    wide_shape = (count, g.rb, g.frames * 3 * g.wide)
    sums_shape = lambda edges: ((3 * SPLIT + edges * g.rb, 128), BF16)

    def over_z(name, stats, send, parts, after):
        near = swap(send, g.inner)
        outs = [stats_shape, sums_shape(parts)]
        total, send = call(g, step_kernel, name, outs, [stats, near], after=after)
        return total, send, [near, swap(send, 2 * g.inner)]

    packed = list(
        call(g, pack_weights_kernel, "pack_weights", [packed_shape], [weights], flops=6 * 10**9)
    )
    for bit in range(g.outer.bit_length() - 1):
        whole = packed[0]
        if bit:
            shape = ((g.wrows << bit, 128), BF16)
            (whole,) = call(g, join_kernel, "join_kernel_rows", [shape], packed)
        packed.append(swap(whole, g.inner << bit))
    sends = call(
        g,
        sort_acts_kernel,
        "sort_acts",
        [block] * g.pairs,
        [acts.reshape(g.cells, g.chans)],
        flops=2*10**9,
    )
    blocks = [sends[0]] + [swap(sends[k], 2 * k) for k in range(1, g.pairs)]
    blocks.append(cross(g, "cross_acts", blocks))
    turned = jnp.swapaxes(cotangent, 2, 3).reshape(g.grows, g.wide)
    direct = [turned] + [swap(turned, 2 * k) for k in range(1, g.pairs)]
    arrived = direct + [swap(v, 1) for v in direct]

    rows, stats, send = call(
        g,
        stats_kernel,
        "stats",
        [((g.inner, g.rb, g.cells), BF16), stats_shape, sums_shape(2)],
        blocks,
        flops=5*10**9,
    )
    kernel_shape = ((g.used, g.outer, g.gp, 256), BF16)
    (rows_of_kernel,) = call(g, prepare_weights_kernel, "kernel_rows", [kernel_shape], packed, flops=7*10**9)
    flops = 2 * 2 * g.inner * 9 * g.rb * 256 * 256 * g.grad_frames
    fields = [
        call(
            g,
            lambda g, *refs, j=j: field_kernel(g, j, *refs),
            "field_grad",
            [(wide_shape, F32)],
            arrived[j * g.pairs : (j + 1) * g.pairs] + [rows_of_kernel],
            flops=flops // 2,
        )[0]
        for j in range(2)
    ]
    stats, _, received = over_z("add_stats", stats, send, 1, ())
    hidden_shape = ((g.outer, count, g.gp, g.cells), BF16)
    normed, hidden, inv, sums, grad, send = call(
        g,
        norm_grad_kernel,
        "norm_grad",
        [rows_shape, hidden_shape, ((g.rb, g.cells), F32), stats_shape, rows_shape, sums_shape(4)],
        [rows, stats, gamma, beta] + fields + received,
        [pltpu.VMEM(*rows_shape), pltpu.VMEM((g.outer, g.gp, g.cells), BF16)],
    )
    half = g.outer // 2
    kept_shape = lambda count: [((count, g.sent, g.outs), F32)] if count else []
    scratch = [
        pltpu.VMEM((half, g.used, g.gp, g.outs), F32),
        pltpu.VMEM((half, count, g.gp, wide_shape[-1]), BF16),
    ]
    (terms,) = call(
        g,
        sent_terms_kernel,
        "sent_terms",
        [((half * g.wrows, 128), BF16)],
        arrived + [hidden],
        scratch,
        flops // 2,
    )
    sums, send, received = over_z("add_sums", sums, send, 2, [terms])
    terms = [swap(terms, g.inner)]
    own, *kept = call(
        g,
        kept_terms_kernel,
        "kept_terms",
        [((g.used * g.gp, g.outs), F32)] + kept_shape(half - 1),
        arrived + [hidden],
        scratch,
        flops // 2,
        after=[send],
    )
    sends = call(
        g,
        finish_kernel,
        "finish",
        [block] * g.pairs,
        [sums, grad, normed, inv] + received,
        after=[own],
    )
    direct = [sends[0]] + [swap(sends[k], 2 * k) for k in range(1, g.pairs)]
    bit = 1
    while kept:
        half //= 2
        send, *kept = call(
            g,
            lambda g, *refs, bit=bit: halve_kernel(g, bit, *refs),
            "halve",
            [((half * g.wrows, 128), BF16)] + kept_shape(half - 1),
            [kept[0], terms[-1]],
        )
        terms.append(swap(send, g.inner << bit))
        bit += 1
    crossed = cross(g, "cross_grads", direct)
    d_acts, d_weights = call(
        g,
        unpack_kernel,
        "unpack",
        [(acts.shape, BF16), (weights.shape, F32)],
        [own] + terms + direct + [crossed],
        [pltpu.VMEM((g.used * g.gp, 128), F32)] * 2,
    )
    if g.blocks > 1:
        d_weights = lax.psum(d_weights, "block")
    return (d_acts, d_weights)


def solution(mesh):
    placed = (
        P("block", "tile", None, None),
        P(),
        P(),
        P("tile", None, None),
        P("block", "tile", None, None),
    )
    return jax.shard_map(
        shards,
        mesh=mesh,
        in_specs=placed,
        out_specs=(P("block", "tile", None, None), P("tile", None, None)),
        check_vma=False,
    )
```

```python
import jax
import jax.numpy as jnp
from jax import lax
from jax.experimental import pallas as pl
from jax.experimental.pallas import tpu as pltpu
from jax.sharding import PartitionSpec as P

GROUPS = 32
norm_eps = 1e-06


F32 = jnp.float32
BF16 = jnp.bfloat16
SPLIT = 16


class Sizes:
    def __init__(self, acts, weights, cotangent, tiles, blocks):
        self.frames, low_rows, self.cols, self.chans = acts.shape
        self.taps, self.outs = weights.shape[1:]
        self.tiles, self.blocks = tiles, blocks
        self.inner = 1 << (tiles.bit_length() // 2)
        self.outer = tiles // self.inner
        self.pairs = self.inner // 2
        self.per = self.chans // GROUPS
        self.gp = 16
        self.rb = self.outer * self.gp
        self.cells = self.frames * self.cols
        self.wide = 2 * self.cols
        self.grad_frames = self.frames * (2 if blocks > 1 else 1)
        self.first = max(0, 3 - self.frames * blocks)
        self.used = 9 * (3 - self.first)
        self.half = -(-self.used * self.per // 32) * 16
        self.sent = 2 * self.half
        self.wrows = self.sent + self.half
        self.lo = 128
        self.hi = self.outs - self.lo
        self.order = [*range(1, self.outer, 2), *range(0, self.outer, 2)]
        self.grows = 2 * self.grad_frames * self.outs
        self.count = float(low_rows * tiles * self.cols * self.per)
        if low_rows != 1 or tiles != GROUPS or self.hi != 64 or self.outer != 4:
            raise ValueError("unsupported sizes")


def swap(value, mask):
    count = lax.axis_size("tile")
    return lax.ppermute(value, "tile", [(i, i ^ mask) for i in range(count)])


def place(g):
    me = lax.axis_index("tile")
    return lax.div(me, g.inner), lax.rem(me, g.inner)


def iota(shape, dim):
    return lax.broadcasted_iota(jnp.int32, shape, dim)


def dot(a, b, dims=((1,), (0,))):
    return lax.dot_general(a, b, (dims, ((), ())), preferred_element_type=F32)


def channel_select(g, w, count):
    shape = (count * g.rb, g.chans)
    row = iota(shape, 0)
    block = row >> (g.rb.bit_length() - 1)
    group = (row & (g.rb - 1)) >> 4
    lane = row & (g.gp - 1)
    chan = g.per * (g.inner * group + (w ^ block)) + lane
    return (chan == iota(shape, 1)) & (lane < g.per)


def column_select(g):
    shape = (g.cells, g.frames * 3 * g.wide)
    row, col = iota(shape, 0), iota(shape, 1)
    bits = g.wide.bit_length() - 1
    part = col >> bits
    frame, shift = part, part
    frame = (part >= 3).astype(jnp.int32)
    for f in range(2, g.frames):
        frame = frame + (part >= 3 * f).astype(jnp.int32)
    shift = part - 3 * frame
    low = ((col & (g.wide - 1)) + shift - 1) >> 1
    inside = (low >= 0) & (low < g.cols)
    return (inside & (low + frame * g.cols == row)).astype(BF16)


def split(value, parts):
    out = []
    for _ in range(parts):
        piece = value.astype(BF16)
        out.append(piece)
        value = value - piece.astype(F32)
    return out


def sort_acts_kernel(g, acts_ref, *out_refs):
    _, w = place(g)
    pick = channel_select(g, w, g.inner).astype(BF16)
    blocks = dot(pick, acts_ref[...], ((1,), (1,))).astype(BF16)
    for k, ref in enumerate(out_refs):
        ref[...] = blocks[2 * k * g.rb : 2 * (k + 1) * g.rb].reshape(2, g.rb, g.cells)


def pack_rows(g, value):
    hi = jnp.concatenate([value[:, g.lo :], jnp.zeros((g.sent, 64), F32)], axis=1)
    lane = iota((g.half, 128), 1)
    both = jnp.where(lane < 64, hi[: g.half], pltpu.roll(hi[g.half :], 64, 1))
    return jnp.concatenate([value[:, : g.lo], both], axis=0).astype(BF16)


def unpack_rows(g, packed):
    both = packed[g.sent :].astype(F32)
    lane = iota(both.shape, 1)
    first = jnp.where(lane < 64, both, 0.0)
    second = jnp.where(lane < 64, pltpu.roll(both, 64, 1), 0.0)
    hi = jnp.concatenate([first, second], axis=0).astype(BF16)
    return jnp.concatenate([packed[: g.sent], hi], axis=1)


def pack_weights_kernel(g, weights_ref, out_ref):
    total = jnp.zeros((g.sent, g.outs), F32)
    row, tap = iota((g.sent, g.taps), 0), iota((g.sent, g.taps), 1) - 9 * g.first
    for i in range(g.per):
        pick = (row == tap * g.per + i) & (tap >= 0)
        total = total + dot(pick.astype(BF16), weights_ref[i])
    out_ref[...] = pack_rows(g, total)


def totals(g, first, second):
    pad = jnp.zeros((8 - g.outer, g.cells), F32)
    out = []
    for value in (first, second):
        out += [jnp.sum(value.reshape(g.outer, g.gp, g.cells), axis=1)]
        if g.outer < 8:
            out += [pad]
    return jnp.concatenate(out, axis=0)


def put_stats(ref, stats):
    for i, piece in enumerate(split(stats, 3)):
        ref[i * SPLIT : (i + 1) * SPLIT] = piece


def send_stats(g, ref, stats, z, rows_ref, parts):
    put_stats(ref, stats)
    last, even = rows_ref.shape[0] - 1, (z & 1) == 0
    for n, row in enumerate((jnp.where(even, last, 0), jnp.where(even, 0, last))):
        edge = rows_ref[row]
        for i, piece in enumerate(split(edge, parts) if parts > 1 else [edge.astype(BF16)]):
            at = 3 * SPLIT + (n * parts + i) * g.rb
            ref[at : at + g.rb] = piece


def step_kernel(g, stats_ref, received_ref, total_ref, send_ref):
    stats = add_stats(stats_ref[...], [received_ref])
    total_ref[...] = stats
    put_stats(send_ref, stats)
    count = send_ref.shape[0] - 3 * SPLIT
    send_ref[3 * SPLIT :] = received_ref[3 * SPLIT + count :]


def edges(g, z, received, parts):
    near, far = (
        sum(
            ref[3 * SPLIT + i * g.rb : 3 * SPLIT + (i + 1) * g.rb].astype(F32)
            for i in range(parts)
        )
        for ref in received
    )
    odd = (z & 1) == 1
    above = jnp.where(odd, near, jnp.where((z ^ 3) == z - 1, far, 0.0))
    below = jnp.where(odd, jnp.where((z ^ 3) == z + 1, far, 0.0), near)
    return above, below


def stats_kernel(g, *refs):
    direct, (crossed, rows_ref, stats_ref, send_ref) = refs[: g.pairs], refs[g.pairs :]
    z, w = place(g)
    first = jnp.zeros((g.rb, g.cells), F32)
    second = jnp.zeros((g.rb, g.cells), F32)
    for k in range(g.pairs):
        for j, block in enumerate((direct[k][0], crossed[k])):
            rows_ref[w ^ (2 * k + j)] = block
            wide = block.astype(F32)
            first = first + wide
            second = second + wide * wide
    stats = totals(g, first, second)
    stats_ref[...] = stats
    send_stats(g, send_ref, stats, z, rows_ref, 1)


def add_stats(own, received):
    for ref in received:
        for i in range(3):
            own = own + ref[i * SPLIT : (i + 1) * SPLIT].astype(F32)
    return own


def spread(g, stats):
    lane = iota((SPLIT, g.cells), 1)
    whole = jnp.zeros((SPLIT, g.cells), F32)
    for t in range(g.frames):
        mine = (lane >= t * g.cols) & (lane < (t + 1) * g.cols)
        part = jnp.sum(jnp.where(mine, stats, 0.0), axis=1, keepdims=True)
        whole = jnp.where(mine, part, whole)
    return tuple(
        jnp.concatenate(
            [
                jnp.broadcast_to(whole[s + q : s + q + 1], (g.gp, g.cells))
                for q in range(g.outer)
            ],
            axis=0,
        )
        for s in (0, 8)
    )


def prepare_weights_kernel(g, *refs):
    *packed, out_ref = refs
    z, _ = place(g)
    shape = (g.used * g.gp, g.sent)
    row, col = iota(shape, 0), iota(shape, 1)
    tap, lane = row >> 4, row & (g.gp - 1)
    pick = ((col == tap * g.per + lane) & (lane < g.per)).astype(BF16)
    blocks = [(ref, at) for ref in packed for at in range(0, ref.shape[0], g.wrows)]
    for k, (ref, at) in enumerate(blocks):
        value = dot(pick, unpack_rows(g, ref[at : at + g.wrows])).astype(BF16)
        out_ref[:, z ^ k] = value.reshape(g.used, g.gp, 256)


def meetings(g, later):
    pairs = [(a, later + a - 2) for a in range(g.first, 3)]
    return [(a, t) for a, t in pairs if 0 <= t < g.frames]


def fine_rows(g, ref, later):
    at = 2 * later * g.outs
    return jnp.concatenate([ref[at : at + g.outs], ref[at + g.outs : at + 2 * g.outs]], axis=1)


def lanes_of(g, t, e):
    return slice((3 * t + e) * g.wide, (3 * t + e + 1) * g.wide)


def field_kernel(g, j, *refs):
    *tiles, weights_ref, field = refs
    _, w = place(g)
    rb, wide = g.rb, g.wide
    field[...] = jnp.zeros_like(field)
    for k, ref in enumerate(tiles):
        row = w ^ (2 * k + j)
        for later in range(g.grad_frames):
            pairs = meetings(g, later)
            if not pairs:
                continue
            low, high = pairs[0][0] - g.first, pairs[-1][0] - g.first + 1
            taps = weights_ref[9 * low : 9 * high].reshape(9 * (high - low) * rb, 256)
            every = dot(taps[:, : g.outs], fine_rows(g, ref, later))
            for n, (_, t) in enumerate(pairs):
                back = every[9 * n * rb : 9 * (n + 1) * rb]
                part = lambda b, e, fine: back[
                    (3 * b + e) * rb : (3 * b + e + 1) * rb, fine * wide : (fine + 1) * wide
                ]
                for e in range(3):
                    lanes = lanes_of(g, t, e)
                    field[row, :, lanes] += part(0, e, 0)
                    field[row + 1, :, lanes] += (part(1, e, 0) + part(2, e, 0)) + (
                        part(0, e, 1) + part(1, e, 1)
                    )
                    field[row + 2, :, lanes] += part(2, e, 1)


def norm_grad_kernel(g, *refs):
    rows_ref, stats_ref, gamma_ref, beta_ref, field_ref, other_ref, *refs = refs
    received, refs = refs[:2], refs[2:]
    normed_ref, hidden_ref, inv_ref, sums_ref, grad_ref, send_ref, slope_ref, hidden_scratch = refs
    z, w = place(g)
    rb = g.rb
    total, total_sq = spread(g, add_stats(stats_ref[...], received[1:]))
    mean = total / g.count
    inv = lax.rsqrt(total_sq / g.count - mean * mean + norm_eps)
    inv_ref[...] = inv
    pick = channel_select(g, w, 1)
    gamma = jnp.sum(jnp.where(pick, gamma_ref[...].reshape(1, g.chans), 0.0), axis=1, keepdims=True)
    beta = jnp.sum(jnp.where(pick, beta_ref[...].reshape(1, g.chans), 0.0), axis=1, keepdims=True)

    def activate(place_at, block, present):
        normed = (block.astype(F32) - mean) * inv
        shifted = normed * gamma + beta
        gate = jax.nn.sigmoid(shifted)
        normed_ref[place_at] = normed
        hidden = (shifted * gate * present).astype(BF16).reshape(g.outer, g.gp, g.cells)
        hidden_scratch[...] = hidden
        for at, k in enumerate(g.order):
            hidden_ref[at, place_at] = hidden_scratch[z ^ k]
        slope_ref[place_at] = gate * (1.0 + shifted * (1.0 - gate)) * gamma * present

    above, below = edges(g, z, received, 1)
    activate(0, above, jnp.where(z > 0, 1.0, 0.0))
    activate(g.inner + 1, below, jnp.where(z < g.outer - 1, 1.0, 0.0))

    @pl.loop(0, g.inner)
    def _(i):
        activate(i + 1, rows_ref[i], 1.0)

    count = g.inner + 2
    select = column_select(g)
    flat = (field_ref[...] + other_ref[...]).reshape(count * rb, g.frames * 3 * g.wide)
    pieces = split(flat, 2)
    act_grad = dot(pieces[0], select, ((1,), (1,))) + dot(pieces[1], select, ((1,), (1,)))
    grad = act_grad.reshape(count, rb, g.cells) * slope_ref[...]
    grad_ref[...] = grad
    sums = totals(g, jnp.sum(grad, axis=0), jnp.sum(grad * normed_ref[...], axis=0))
    sums_ref[...] = sums
    send_stats(g, send_ref, sums, z, grad_ref, 2)


def kernel_terms(g, first, direct, crossed, hidden_ref, acc, ups):
    _, w = place(g)
    part = acc.shape[0]
    flat = hidden_ref[first : first + part].reshape(-1, g.cells)
    ups[...] = dot(flat, column_select(g)).astype(BF16).reshape(ups.shape)
    started = set()
    for later in range(g.grad_frames):
        for a, t in meetings(g, later):
            left, right = [], []
            for k in range(g.pairs):
                for j, ref in enumerate((direct[k], crossed[k])):
                    row = w ^ (2 * k + j)
                    pieces = []
                    for group in range(part):
                        for upper, lower in ((0, 1), (1, 1), (1, 2)):
                            for e in range(3):
                                lanes = lanes_of(g, t, e)
                                sides = [ups[group, row + at, :, lanes] for at in (upper, lower)]
                                pieces.append(jnp.concatenate(sides, axis=1))
                    left.append(jnp.concatenate(pieces, axis=0))
                    right.append(fine_rows(g, ref, later))
            terms = dot(
                jnp.concatenate(left, axis=1), jnp.concatenate(right, axis=1), ((1,), (1,))
            ).reshape(part, 9, g.gp, g.outs)
            taps = slice(9 * (a - g.first), 9 * (a - g.first + 1))
            if a in started:
                acc[:, taps] += terms
            else:
                acc[:, taps] = terms
                started.add(a)


def sent_order(g):
    shape = (g.sent, g.used * g.gp)
    row, col = iota(shape, 0), iota(shape, 1)
    tap, lane = col >> 4, col & (g.gp - 1)
    return ((row == tap * g.per + lane) & (lane < g.per)).astype(BF16)


def sent_terms_kernel(g, *refs):
    direct, crossed, refs = refs[: g.pairs], refs[g.pairs : 2 * g.pairs], refs[2 * g.pairs :]
    hidden_ref, send_ref, acc, ups = refs
    kernel_terms(g, 0, direct, crossed, hidden_ref, acc, ups)
    pick = sent_order(g)
    for i in range(g.outer // 2):
        terms = acc[i].reshape(g.used * g.gp, g.outs).astype(BF16)
        send_ref[i * g.wrows : (i + 1) * g.wrows] = pack_rows(g, dot(pick, terms))


def kept_terms_kernel(g, *refs):
    direct, crossed, refs = refs[: g.pairs], refs[g.pairs : 2 * g.pairs], refs[2 * g.pairs :]
    hidden_ref, own_ref, *kept, acc, ups = refs
    kernel_terms(g, g.outer // 2, direct, crossed, hidden_ref, acc, ups)
    own_ref[...] = acc[0].reshape(g.used * g.gp, g.outs)
    pick = sent_order(g)
    for i in range(1, g.outer // 2):
        terms = acc[i].reshape(g.used * g.gp, g.outs)
        kept[0][i - 1] = sum(dot(pick, piece) for piece in split(terms, 2))


def halve_kernel(g, bit, keep_ref, received_ref, *refs):
    send_ref, *kept = refs
    for i in range(keep_ref.shape[0]):
        block = received_ref[(i + 1) * g.wrows : (i + 2) * g.wrows]
        total = keep_ref[i] + unpack_rows(g, block).astype(F32)[:, : g.outs]
        if i % 2:
            kept[0][i // 2] = total
        else:
            send_ref[i // 2 * g.wrows : (i // 2 + 1) * g.wrows] = pack_rows(g, total)


def finish_kernel(g, *refs):
    sums_ref, grad_ref, normed_ref, inv_ref, *refs = refs
    received, sends = refs[:2], refs[2:]
    z, w = place(g)
    first, second = spread(g, add_stats(sums_ref[...], received[1:]))
    first, second = first / g.count, second / g.count
    inv = inv_ref[...]
    above, below = edges(g, z, received, 2)
    for k, ref in enumerate(sends):
        for j in range(2):
            row = w ^ (2 * k + j)
            grad = grad_ref[row + 1]
            grad = grad + jnp.where(row == 0, above, 0.0)
            grad = grad + jnp.where(row == g.inner - 1, below, 0.0)
            ref[j] = (inv * (grad - first - normed_ref[row + 1] * second)).astype(BF16)


STEP = 32


def in_order(g, received):
    shape = (g.per * STEP, g.sent)
    row, col = iota(shape, 0), iota(shape, 1)
    tap, lane = row & (STEP - 1), row >> 5
    pick = ((col == tap * g.per + lane) & (tap < g.used)).astype(BF16)
    return sum(dot(pick, unpack_rows(g, ref[: g.wrows])) for ref in received)


def unpack_acts_kernel(g, own_ref, near_ref, *refs):
    direct, (crossed, acts_ref, part_ref, low, high) = refs[: g.pairs], refs[g.pairs :]
    _, w = place(g)
    pick = channel_select(g, w, g.inner).astype(BF16)
    blocks = []
    for k in range(g.pairs):
        blocks += [direct[k][0], crossed[k]]
    d_acts = dot(jnp.concatenate(blocks, axis=0), pick, ((0,), (0,)))
    acts_ref[...] = d_acts.astype(BF16).reshape(acts_ref.shape)
    total = in_order(g, [near_ref])
    low[...] = own_ref[:, : g.lo]
    high[:, : g.hi] = own_ref[:, g.lo :]
    for i in range(g.per):
        at = pl.ds(i, g.used, stride=g.gp)
        there = total[i * STEP : i * STEP + g.used]
        part_ref[i, : g.used, : g.lo] = low[at, :] + there[:, : g.lo]
        part_ref[i, : g.used, g.lo :] = high[at, :][:, : g.hi] + there[:, g.lo : g.outs]


def unpack_weights_kernel(g, part_ref, *refs):
    *received, out_ref = refs
    total = in_order(g, received)
    for i in range(g.per):
        if g.first:
            out_ref[i, : 9 * g.first, :] = jnp.zeros((9 * g.first, g.outs), F32)
        there = total[i * STEP : i * STEP + g.used, : g.outs]
        out_ref[i, 9 * g.first :, :] = part_ref[i, : g.used, :] + there


def call(g, kernel, name, outs, args, scratch=(), flops=0, after=()):
    shapes = [jax.ShapeDtypeStruct(shape, kind) for shape, kind in outs]
    whole = pl.BlockSpec(memory_space=pltpu.VMEM)
    moved = sum(a.size * a.dtype.itemsize for a in list(args) + shapes)
    count = len(args)
    rest = count + len(after)
    return pl.pallas_call(
        lambda *refs: kernel(g, *refs[:count], *refs[rest:]),
        out_shape=shapes,
        in_specs=[whole] * count + [pl.BlockSpec(memory_space=pl.ANY)] * len(after),
        out_specs=[whole] * len(shapes),
        scratch_shapes=list(scratch),
        compiler_params=pltpu.CompilerParams(vmem_limit_bytes=48 * 1024 * 1024),
        cost_estimate=pl.CostEstimate(flops=flops, bytes_accessed=moved, transcendentals=0),
        name=name,
    )(*args, *after)


def copy_kernel(g, in_ref, out_ref):
    out_ref[...] = in_ref[...]


def join_kernel(g, *refs):
    *parts, out_ref = refs
    at = 0
    for ref in parts:
        out_ref[at : at + ref.shape[0]] = ref[...]
        at += ref.shape[0]


def pass_on(g, value, after):
    return call(g, copy_kernel, "pass_on", [(value.shape, value.dtype)], [value], after=after)[0]


def cross_kernel(g, *refs):
    *blocks, out_ref = refs
    for k, ref in enumerate(blocks):
        out_ref[k] = ref[1]


def cross(g, name, direct):
    shape = (g.pairs, g.rb, g.cells)
    (out,) = call(g, cross_kernel, name, [(shape, BF16)], direct)
    return swap(out, 1)


def shards(acts, gamma, beta, weights, cotangent):
    g = Sizes(acts, weights, cotangent, lax.axis_size("tile"), lax.axis_size("block"))
    if g.blocks > 1:
        pairs = [(i + 1, i) for i in range(g.blocks - 1)]
        following = lax.ppermute(cotangent, "block", pairs)
        cotangent = jnp.concatenate([cotangent, following], 0)
    count = g.inner + 2
    block = ((2, g.rb, g.cells), BF16)
    rows_shape = ((count, g.rb, g.cells), F32)
    stats_shape = ((SPLIT, g.cells), F32)
    packed_shape = ((g.wrows, 128), BF16)
    wide_shape = (count, g.rb, g.frames * 3 * g.wide)
    sums_shape = lambda edges: ((3 * SPLIT + edges * g.rb, 128), BF16)

    def over_z(name, stats, send, parts, after):
        near = swap(send, g.inner)
        outs = [stats_shape, sums_shape(parts)]
        total, send = call(g, step_kernel, name, outs, [stats, near], after=after)
        return total, send, [near, swap(send, 2 * g.inner)]

    packed = list(
        call(g, pack_weights_kernel, "pack_weights", [packed_shape], [weights], flops=6 * 10**9)
    )
    for bit in range(g.outer.bit_length() - 1):
        whole = packed[0]
        if bit:
            shape = ((g.wrows << bit, 128), BF16)
            (whole,) = call(g, join_kernel, "join_kernel_rows", [shape], packed)
        packed.append(swap(whole, g.inner << bit))
    sends = call(
        g,
        sort_acts_kernel,
        "sort_acts",
        [block] * g.pairs,
        [acts.reshape(g.cells, g.chans)],
        flops=2*10**9,
    )
    blocks = [sends[0]] + [swap(sends[k], 2 * k) for k in range(1, g.pairs)]
    blocks.append(cross(g, "cross_acts", blocks))
    turned = jnp.swapaxes(cotangent, 2, 3).reshape(g.grows, g.wide)
    direct = [turned] + [swap(turned, 2 * k) for k in range(1, g.pairs)]
    arrived = direct + [swap(v, 1) for v in direct]

    rows, stats, send = call(
        g,
        stats_kernel,
        "stats",
        [((g.inner, g.rb, g.cells), BF16), stats_shape, sums_shape(2)],
        blocks,
        flops=5*10**9,
    )
    kernel_shape = ((g.used, g.outer, g.gp, 256), BF16)
    (rows_of_kernel,) = call(g, prepare_weights_kernel, "kernel_rows", [kernel_shape], packed, flops=7*10**9)
    flops = 2 * 2 * g.inner * 9 * g.rb * 256 * 256 * g.grad_frames
    fields = [
        call(
            g,
            lambda g, *refs, j=j: field_kernel(g, j, *refs),
            "field_grad",
            [(wide_shape, F32)],
            arrived[j * g.pairs : (j + 1) * g.pairs] + [rows_of_kernel],
            flops=flops // 2,
        )[0]
        for j in range(2)
    ]
    stats, _, received = over_z("add_stats", stats, send, 1, ())
    hidden_shape = ((g.outer, count, g.gp, g.cells), BF16)
    normed, hidden, inv, sums, grad, send = call(
        g,
        norm_grad_kernel,
        "norm_grad",
        [rows_shape, hidden_shape, ((g.rb, g.cells), F32), stats_shape, rows_shape, sums_shape(4)],
        [rows, stats, gamma, beta] + fields + received,
        [pltpu.VMEM(*rows_shape), pltpu.VMEM((g.outer, g.gp, g.cells), BF16)],
    )
    half = g.outer // 2
    kept_shape = lambda count: [((count, g.sent, g.outs), F32)] if count else []
    scratch = [
        pltpu.VMEM((half, g.used, g.gp, g.outs), F32),
        pltpu.VMEM((half, count, g.gp, wide_shape[-1]), BF16),
    ]
    (terms,) = call(
        g,
        sent_terms_kernel,
        "sent_terms",
        [((half * g.wrows, 128), BF16)],
        arrived + [hidden],
        scratch,
        flops // 2,
    )
    sums, send, received = over_z("add_sums", sums, send, 2, [terms])
    terms = [swap(terms, g.inner)]
    own, *kept = call(
        g,
        kept_terms_kernel,
        "kept_terms",
        [((g.used * g.gp, g.outs), F32)] + kept_shape(half - 1),
        arrived + [hidden],
        scratch,
        flops // 2,
        after=[send],
    )
    sends = call(
        g,
        finish_kernel,
        "finish",
        [block] * g.pairs,
        [sums, grad, normed, inv] + received,
        after=[own],
    )
    direct = [sends[0]] + [swap(sends[k], 2 * k) for k in range(1, g.pairs)]
    bit = 1
    while kept:
        half //= 2
        send, *kept = call(
            g,
            lambda g, *refs, bit=bit: halve_kernel(g, bit, *refs),
            "halve",
            [((half * g.wrows, 128), BF16)] + kept_shape(half - 1),
            [kept[0], terms[-1]],
        )
        terms.append(swap(send, g.inner << bit))
        bit += 1
    crossed = cross(g, "cross_grads", direct)
    d_acts, part = call(
        g,
        unpack_acts_kernel,
        "unpack_acts",
        [(acts.shape, BF16), ((g.per, STEP, g.outs), F32)],
        [own, terms[0]] + direct + [crossed],
        [pltpu.VMEM((g.used * g.gp, 128), F32)] * 2,
    )
    (d_weights,) = call(
        g, unpack_weights_kernel, "unpack_weights", [(weights.shape, F32)], [part] + terms[1:]
    )
    if g.blocks > 1:
        d_weights = lax.psum(d_weights, "block")
    return (d_acts, d_weights)


def solution(mesh):
    placed = (
        P("block", "tile", None, None),
        P(),
        P(),
        P("tile", None, None),
        P("block", "tile", None, None),
    )
    return jax.shard_map(
        shards,
        mesh=mesh,
        in_specs=placed,
        out_specs=(P("block", "tile", None, None), P("tile", None, None)),
        check_vma=False,
    )
```

```python
import jax
import jax.numpy as jnp
from jax import lax
from jax.experimental import pallas as pl
from jax.experimental.pallas import tpu as pltpu
from jax.sharding import PartitionSpec as P

GROUPS = 32
norm_eps = 1e-06


F32 = jnp.float32
BF16 = jnp.bfloat16
SPLIT = 16


class Sizes:
    def __init__(self, acts, weights, cotangent, tiles, blocks):
        self.frames, low_rows, self.cols, self.chans = acts.shape
        self.taps, self.outs = weights.shape[1:]
        self.tiles, self.blocks = tiles, blocks
        self.inner = 1 << (tiles.bit_length() // 2)
        self.outer = tiles // self.inner
        self.pairs = self.inner // 2
        self.per = self.chans // GROUPS
        self.gp = 16
        self.rb = self.outer * self.gp
        self.cells = self.frames * self.cols
        self.wide = 2 * self.cols
        self.grad_frames = self.frames * (2 if blocks > 1 else 1)
        self.first = max(0, 3 - self.frames * blocks)
        self.used = 9 * (3 - self.first)
        self.half = -(-self.used * self.per // 32) * 16
        self.sent = 2 * self.half
        self.wrows = self.sent + self.half
        self.lo = 128
        self.hi = self.outs - self.lo
        self.order = [*range(1, self.outer, 2), *range(0, self.outer, 2)]
        self.grows = 2 * self.grad_frames * self.outs
        self.count = float(low_rows * tiles * self.cols * self.per)
        if low_rows != 1 or tiles != GROUPS or self.hi != 64 or self.outer != 4:
            raise ValueError("unsupported sizes")


def swap(value, mask):
    count = lax.axis_size("tile")
    return lax.ppermute(value, "tile", [(i, i ^ mask) for i in range(count)])


def place(g):
    me = lax.axis_index("tile")
    return lax.div(me, g.inner), lax.rem(me, g.inner)


def iota(shape, dim):
    return lax.broadcasted_iota(jnp.int32, shape, dim)


def dot(a, b, dims=((1,), (0,))):
    return lax.dot_general(a, b, (dims, ((), ())), preferred_element_type=F32)


def channel_select(g, w, count):
    shape = (count * g.rb, g.chans)
    row = iota(shape, 0)
    block = row >> (g.rb.bit_length() - 1)
    group = (row & (g.rb - 1)) >> 4
    lane = row & (g.gp - 1)
    chan = g.per * (g.inner * group + (w ^ block)) + lane
    return (chan == iota(shape, 1)) & (lane < g.per)


def column_select(g):
    shape = (g.cells, g.frames * 3 * g.wide)
    row, col = iota(shape, 0), iota(shape, 1)
    bits = g.wide.bit_length() - 1
    part = col >> bits
    frame, shift = part, part
    frame = (part >= 3).astype(jnp.int32)
    for f in range(2, g.frames):
        frame = frame + (part >= 3 * f).astype(jnp.int32)
    shift = part - 3 * frame
    low = ((col & (g.wide - 1)) + shift - 1) >> 1
    inside = (low >= 0) & (low < g.cols)
    return (inside & (low + frame * g.cols == row)).astype(BF16)


def split(value, parts):
    out = []
    for _ in range(parts):
        piece = value.astype(BF16)
        out.append(piece)
        value = value - piece.astype(F32)
    return out


def sort_acts_kernel(g, acts_ref, *out_refs):
    _, w = place(g)
    pick = channel_select(g, w, g.inner).astype(BF16)
    blocks = dot(pick, acts_ref[...], ((1,), (1,))).astype(BF16)
    for k, ref in enumerate(out_refs):
        ref[...] = blocks[2 * k * g.rb : 2 * (k + 1) * g.rb].reshape(2, g.rb, g.cells)


def pack_rows(g, value):
    hi = jnp.concatenate([value[:, g.lo :], jnp.zeros((g.sent, 64), F32)], axis=1)
    lane = iota((g.half, 128), 1)
    both = jnp.where(lane < 64, hi[: g.half], pltpu.roll(hi[g.half :], 64, 1))
    return jnp.concatenate([value[:, : g.lo], both], axis=0).astype(BF16)


def unpack_rows(g, packed):
    both = packed[g.sent :].astype(F32)
    lane = iota(both.shape, 1)
    first = jnp.where(lane < 64, both, 0.0)
    second = jnp.where(lane < 64, pltpu.roll(both, 64, 1), 0.0)
    hi = jnp.concatenate([first, second], axis=0).astype(BF16)
    return jnp.concatenate([packed[: g.sent], hi], axis=1)


def pack_weights_kernel(g, weights_ref, out_ref):
    total = jnp.zeros((g.sent, g.outs), F32)
    row, tap = iota((g.sent, g.taps), 0), iota((g.sent, g.taps), 1) - 9 * g.first
    for i in range(g.per):
        pick = (row == tap * g.per + i) & (tap >= 0)
        total = total + dot(pick.astype(BF16), weights_ref[i])
    out_ref[...] = pack_rows(g, total)


def totals(g, first, second):
    pad = jnp.zeros((8 - g.outer, g.cells), F32)
    out = []
    for value in (first, second):
        out += [jnp.sum(value.reshape(g.outer, g.gp, g.cells), axis=1)]
        if g.outer < 8:
            out += [pad]
    return jnp.concatenate(out, axis=0)


def put_stats(ref, stats):
    for i, piece in enumerate(split(stats, 3)):
        ref[i * SPLIT : (i + 1) * SPLIT] = piece


def send_stats(g, ref, stats, z, rows_ref, parts):
    put_stats(ref, stats)
    last, even = rows_ref.shape[0] - 1, (z & 1) == 0
    for n, row in enumerate((jnp.where(even, last, 0), jnp.where(even, 0, last))):
        edge = rows_ref[row]
        for i, piece in enumerate(split(edge, parts) if parts > 1 else [edge.astype(BF16)]):
            at = 3 * SPLIT + (n * parts + i) * g.rb
            ref[at : at + g.rb] = piece


def step_kernel(g, stats_ref, received_ref, total_ref, send_ref):
    stats = add_stats(stats_ref[...], [received_ref])
    total_ref[...] = stats
    put_stats(send_ref, stats)
    count = send_ref.shape[0] - 3 * SPLIT
    send_ref[3 * SPLIT :] = received_ref[3 * SPLIT + count :]


def edges(g, z, received, parts):
    near, far = (
        sum(
            ref[3 * SPLIT + i * g.rb : 3 * SPLIT + (i + 1) * g.rb].astype(F32)
            for i in range(parts)
        )
        for ref in received
    )
    odd = (z & 1) == 1
    above = jnp.where(odd, near, jnp.where((z ^ 3) == z - 1, far, 0.0))
    below = jnp.where(odd, jnp.where((z ^ 3) == z + 1, far, 0.0), near)
    return above, below


def stats_kernel(g, *refs):
    direct, (crossed, rows_ref, stats_ref, send_ref) = refs[: g.pairs], refs[g.pairs :]
    z, w = place(g)
    first = jnp.zeros((g.rb, g.cells), F32)
    second = jnp.zeros((g.rb, g.cells), F32)
    for k in range(g.pairs):
        for j, block in enumerate((direct[k][0], crossed[k])):
            rows_ref[w ^ (2 * k + j)] = block
            wide = block.astype(F32)
            first = first + wide
            second = second + wide * wide
    stats = totals(g, first, second)
    stats_ref[...] = stats
    send_stats(g, send_ref, stats, z, rows_ref, 1)


def add_stats(own, received):
    for ref in received:
        for i in range(3):
            own = own + ref[i * SPLIT : (i + 1) * SPLIT].astype(F32)
    return own


def spread(g, stats):
    lane = iota((SPLIT, g.cells), 1)
    whole = jnp.zeros((SPLIT, g.cells), F32)
    for t in range(g.frames):
        mine = (lane >= t * g.cols) & (lane < (t + 1) * g.cols)
        part = jnp.sum(jnp.where(mine, stats, 0.0), axis=1, keepdims=True)
        whole = jnp.where(mine, part, whole)
    return tuple(
        jnp.concatenate(
            [
                jnp.broadcast_to(whole[s + q : s + q + 1], (g.gp, g.cells))
                for q in range(g.outer)
            ],
            axis=0,
        )
        for s in (0, 8)
    )


def prepare_weights_kernel(g, *refs):
    *packed, out_ref = refs
    z, _ = place(g)
    shape = (g.used * g.gp, g.sent)
    row, col = iota(shape, 0), iota(shape, 1)
    tap, lane = row >> 4, row & (g.gp - 1)
    pick = ((col == tap * g.per + lane) & (lane < g.per)).astype(BF16)
    blocks = [(ref, at) for ref in packed for at in range(0, ref.shape[0], g.wrows)]
    for k, (ref, at) in enumerate(blocks):
        value = dot(pick, unpack_rows(g, ref[at : at + g.wrows])).astype(BF16)
        out_ref[:, z ^ k] = value.reshape(g.used, g.gp, 256)


def meetings(g, later):
    pairs = [(a, later + a - 2) for a in range(g.first, 3)]
    return [(a, t) for a, t in pairs if 0 <= t < g.frames]


def fine_rows(g, ref, later):
    at = 2 * later * g.outs
    return jnp.concatenate([ref[at : at + g.outs], ref[at + g.outs : at + 2 * g.outs]], axis=1)


def lanes_of(g, t, e):
    return slice((3 * t + e) * g.wide, (3 * t + e + 1) * g.wide)


def field_kernel(g, j, *refs):
    *tiles, weights_ref, field = refs
    _, w = place(g)
    rb, wide = g.rb, g.wide
    field[...] = jnp.zeros_like(field)
    for k, ref in enumerate(tiles):
        row = w ^ (2 * k + j)
        for later in range(g.grad_frames):
            pairs = meetings(g, later)
            if not pairs:
                continue
            low, high = pairs[0][0] - g.first, pairs[-1][0] - g.first + 1
            taps = weights_ref[9 * low : 9 * high].reshape(9 * (high - low) * rb, 256)
            every = dot(taps[:, : g.outs], fine_rows(g, ref, later))
            for n, (_, t) in enumerate(pairs):
                back = every[9 * n * rb : 9 * (n + 1) * rb]
                part = lambda b, e, fine: back[
                    (3 * b + e) * rb : (3 * b + e + 1) * rb, fine * wide : (fine + 1) * wide
                ]
                for e in range(3):
                    lanes = lanes_of(g, t, e)
                    field[row, :, lanes] += part(0, e, 0)
                    field[row + 1, :, lanes] += (part(1, e, 0) + part(2, e, 0)) + (
                        part(0, e, 1) + part(1, e, 1)
                    )
                    field[row + 2, :, lanes] += part(2, e, 1)


def norm_grad_kernel(g, *refs):
    rows_ref, stats_ref, gamma_ref, beta_ref, field_ref, other_ref, *refs = refs
    received, refs = refs[:2], refs[2:]
    normed_ref, hidden_ref, inv_ref, sums_ref, grad_ref, send_ref, slope_ref, hidden_scratch = refs
    z, w = place(g)
    rb = g.rb
    total, total_sq = spread(g, add_stats(stats_ref[...], received[1:]))
    mean = total / g.count
    inv = lax.rsqrt(total_sq / g.count - mean * mean + norm_eps)
    inv_ref[...] = inv
    pick = channel_select(g, w, 1)
    gamma = jnp.sum(jnp.where(pick, gamma_ref[...].reshape(1, g.chans), 0.0), axis=1, keepdims=True)
    beta = jnp.sum(jnp.where(pick, beta_ref[...].reshape(1, g.chans), 0.0), axis=1, keepdims=True)

    def activate(place_at, block, present):
        normed = (block.astype(F32) - mean) * inv
        shifted = normed * gamma + beta
        gate = jax.nn.sigmoid(shifted)
        normed_ref[place_at] = normed
        hidden = (shifted * gate * present).astype(BF16).reshape(g.outer, g.gp, g.cells)
        hidden_scratch[...] = hidden
        for at, k in enumerate(g.order):
            hidden_ref[at, place_at] = hidden_scratch[z ^ k]
        slope_ref[place_at] = gate * (1.0 + shifted * (1.0 - gate)) * gamma * present

    above, below = edges(g, z, received, 1)
    activate(0, above, jnp.where(z > 0, 1.0, 0.0))
    activate(g.inner + 1, below, jnp.where(z < g.outer - 1, 1.0, 0.0))

    @pl.loop(0, g.inner)
    def _(i):
        activate(i + 1, rows_ref[i], 1.0)

    count = g.inner + 2
    select = column_select(g)
    flat = (field_ref[...] + other_ref[...]).reshape(count * rb, g.frames * 3 * g.wide)
    pieces = split(flat, 2)
    act_grad = dot(pieces[0], select, ((1,), (1,))) + dot(pieces[1], select, ((1,), (1,)))
    grad = act_grad.reshape(count, rb, g.cells) * slope_ref[...]
    grad_ref[...] = grad
    sums = totals(g, jnp.sum(grad, axis=0), jnp.sum(grad * normed_ref[...], axis=0))
    sums_ref[...] = sums
    send_stats(g, send_ref, sums, z, grad_ref, 1)


def kernel_terms(g, first, direct, crossed, hidden_ref, acc, ups):
    _, w = place(g)
    part = acc.shape[0]
    flat = hidden_ref[first : first + part].reshape(-1, g.cells)
    ups[...] = dot(flat, column_select(g)).astype(BF16).reshape(ups.shape)
    started = set()
    for later in range(g.grad_frames):
        for a, t in meetings(g, later):
            left, right = [], []
            for k in range(g.pairs):
                for j, ref in enumerate((direct[k], crossed[k])):
                    row = w ^ (2 * k + j)
                    pieces = []
                    for group in range(part):
                        for upper, lower in ((0, 1), (1, 1), (1, 2)):
                            for e in range(3):
                                lanes = lanes_of(g, t, e)
                                sides = [ups[group, row + at, :, lanes] for at in (upper, lower)]
                                pieces.append(jnp.concatenate(sides, axis=1))
                    left.append(jnp.concatenate(pieces, axis=0))
                    right.append(fine_rows(g, ref, later))
            terms = dot(
                jnp.concatenate(left, axis=1), jnp.concatenate(right, axis=1), ((1,), (1,))
            ).reshape(part, 9, g.gp, g.outs)
            taps = slice(9 * (a - g.first), 9 * (a - g.first + 1))
            if a in started:
                acc[:, taps] += terms
            else:
                acc[:, taps] = terms
                started.add(a)


def sent_order(g):
    shape = (g.sent, g.used * g.gp)
    row, col = iota(shape, 0), iota(shape, 1)
    tap, lane = col >> 4, col & (g.gp - 1)
    return ((row == tap * g.per + lane) & (lane < g.per)).astype(BF16)


def sent_terms_kernel(g, *refs):
    direct, crossed, refs = refs[: g.pairs], refs[g.pairs : 2 * g.pairs], refs[2 * g.pairs :]
    hidden_ref, *sends, acc, ups = refs
    kernel_terms(g, 0, direct, crossed, hidden_ref, acc, ups)
    pick = sent_order(g)
    for i, ref in enumerate(sends):
        terms = acc[i].reshape(g.used * g.gp, g.outs).astype(BF16)
        ref[...] = pack_rows(g, dot(pick, terms))


def kept_terms_kernel(g, *refs):
    direct, crossed, refs = refs[: g.pairs], refs[g.pairs : 2 * g.pairs], refs[2 * g.pairs :]
    hidden_ref, own_ref, keep_ref, acc, ups = refs
    kernel_terms(g, g.outer // 2, direct, crossed, hidden_ref, acc, ups)
    own_ref[...] = acc[0].reshape(g.used * g.gp, g.outs)
    pick = sent_order(g)
    terms = acc[1].reshape(g.used * g.gp, g.outs)
    keep_ref[...] = sum(dot(pick, piece) for piece in split(terms, 2))


def add_terms_kernel(g, keep_ref, received_ref, send_ref):
    block = unpack_rows(g, received_ref[...]).astype(F32)
    send_ref[...] = pack_rows(g, keep_ref[...] + block[:, : g.outs])


def finish_kernel(g, *refs):
    sums_ref, grad_ref, normed_ref, inv_ref, *refs = refs
    received, sends = refs[:2], refs[2:]
    z, w = place(g)
    first, second = spread(g, add_stats(sums_ref[...], received[1:]))
    first, second = first / g.count, second / g.count
    inv = inv_ref[...]
    above, below = edges(g, z, received, 1)
    for k, ref in enumerate(sends):
        for j in range(2):
            row = w ^ (2 * k + j)
            grad = grad_ref[row + 1]
            grad = grad + jnp.where(row == 0, above, 0.0)
            grad = grad + jnp.where(row == g.inner - 1, below, 0.0)
            ref[j] = (inv * (grad - first - normed_ref[row + 1] * second)).astype(BF16)


STEP = 32


def in_order(g, received):
    shape = (g.per * STEP, g.sent)
    row, col = iota(shape, 0), iota(shape, 1)
    tap, lane = row & (STEP - 1), row >> 5
    pick = ((col == tap * g.per + lane) & (tap < g.used)).astype(BF16)
    return sum(dot(pick, unpack_rows(g, ref[: g.wrows])) for ref in received)


def unpack_acts_kernel(g, own_ref, near_ref, *refs):
    direct, (crossed, acts_ref, part_ref, low, high) = refs[: g.pairs], refs[g.pairs :]
    _, w = place(g)
    pick = channel_select(g, w, g.inner).astype(BF16)
    blocks = []
    for k in range(g.pairs):
        blocks += [direct[k][0], crossed[k]]
    d_acts = dot(jnp.concatenate(blocks, axis=0), pick, ((0,), (0,)))
    acts_ref[...] = d_acts.astype(BF16).reshape(acts_ref.shape)
    total = in_order(g, [near_ref])
    low[...] = own_ref[:, : g.lo]
    high[:, : g.hi] = own_ref[:, g.lo :]
    for i in range(g.per):
        at = pl.ds(i, g.used, stride=g.gp)
        there = total[i * STEP : i * STEP + g.used]
        part_ref[i, : g.used, : g.lo] = low[at, :] + there[:, : g.lo]
        part_ref[i, : g.used, g.lo :] = high[at, :][:, : g.hi] + there[:, g.lo : g.outs]


def unpack_weights_kernel(g, part_ref, *refs):
    *received, out_ref = refs
    total = in_order(g, received)
    for i in range(g.per):
        if g.first:
            out_ref[i, : 9 * g.first, :] = jnp.zeros((9 * g.first, g.outs), F32)
        there = total[i * STEP : i * STEP + g.used, : g.outs]
        out_ref[i, 9 * g.first :, :] = part_ref[i, : g.used, :] + there


def call(g, kernel, name, outs, args, scratch=(), flops=0, after=()):
    shapes = [jax.ShapeDtypeStruct(shape, kind) for shape, kind in outs]
    whole = pl.BlockSpec(memory_space=pltpu.VMEM)
    moved = sum(a.size * a.dtype.itemsize for a in list(args) + shapes)
    count = len(args)
    rest = count + len(after)
    return pl.pallas_call(
        lambda *refs: kernel(g, *refs[:count], *refs[rest:]),
        out_shape=shapes,
        in_specs=[whole] * count + [pl.BlockSpec(memory_space=pl.ANY)] * len(after),
        out_specs=[whole] * len(shapes),
        scratch_shapes=list(scratch),
        compiler_params=pltpu.CompilerParams(vmem_limit_bytes=48 * 1024 * 1024),
        cost_estimate=pl.CostEstimate(flops=flops, bytes_accessed=moved, transcendentals=0),
        name=name,
    )(*args, *after)


def copy_kernel(g, in_ref, out_ref):
    out_ref[...] = in_ref[...]


def join_kernel(g, *refs):
    *parts, out_ref = refs
    at = 0
    for ref in parts:
        out_ref[at : at + ref.shape[0]] = ref[...]
        at += ref.shape[0]


def pass_on(g, value, after):
    return call(g, copy_kernel, "pass_on", [(value.shape, value.dtype)], [value], after=after)[0]


def cross_kernel(g, *refs):
    *blocks, out_ref = refs
    for k, ref in enumerate(blocks):
        out_ref[k] = ref[1]


def cross(g, name, direct):
    shape = (g.pairs, g.rb, g.cells)
    (out,) = call(g, cross_kernel, name, [(shape, BF16)], direct)
    return swap(out, 1)


def shards(acts, gamma, beta, weights, cotangent):
    g = Sizes(acts, weights, cotangent, lax.axis_size("tile"), lax.axis_size("block"))
    if g.blocks > 1:
        pairs = [(i + 1, i) for i in range(g.blocks - 1)]
        following = lax.ppermute(cotangent, "block", pairs)
        cotangent = jnp.concatenate([cotangent, following], 0)
    count = g.inner + 2
    block = ((2, g.rb, g.cells), BF16)
    rows_shape = ((count, g.rb, g.cells), F32)
    stats_shape = ((SPLIT, g.cells), F32)
    packed_shape = ((g.wrows, 128), BF16)
    wide_shape = (count, g.rb, g.frames * 3 * g.wide)
    sums_shape = lambda edges: ((3 * SPLIT + edges * g.rb, 128), BF16)

    def over_z(name, stats, send, parts, after):
        near = swap(send, g.inner)
        outs = [stats_shape, sums_shape(parts)]
        total, send = call(g, step_kernel, name, outs, [stats, near], after=after)
        return total, send, [near, swap(send, 2 * g.inner)]

    packed = list(
        call(g, pack_weights_kernel, "pack_weights", [packed_shape], [weights], flops=6 * 10**9)
    )
    for bit in range(g.outer.bit_length() - 1):
        whole = packed[0]
        if bit:
            shape = ((g.wrows << bit, 128), BF16)
            (whole,) = call(g, join_kernel, "join_kernel_rows", [shape], packed)
        packed.append(swap(whole, g.inner << bit))
    sends = call(
        g,
        sort_acts_kernel,
        "sort_acts",
        [block] * g.pairs,
        [acts.reshape(g.cells, g.chans)],
        flops=2*10**9,
    )
    blocks = [sends[0]] + [swap(sends[k], 2 * k) for k in range(1, g.pairs)]
    blocks.append(cross(g, "cross_acts", blocks))
    turned = jnp.swapaxes(cotangent, 2, 3).reshape(g.grows, g.wide)
    direct = [turned] + [swap(turned, 2 * k) for k in range(1, g.pairs)]
    arrived = direct + [swap(v, 1) for v in direct]

    rows, stats, send = call(
        g,
        stats_kernel,
        "stats",
        [((g.inner, g.rb, g.cells), BF16), stats_shape, sums_shape(2)],
        blocks,
        flops=5*10**9,
    )
    kernel_shape = ((g.used, g.outer, g.gp, 256), BF16)
    (rows_of_kernel,) = call(g, prepare_weights_kernel, "kernel_rows", [kernel_shape], packed, flops=7*10**9)
    flops = 2 * 2 * g.inner * 9 * g.rb * 256 * 256 * g.grad_frames
    fields = [
        call(
            g,
            lambda g, *refs, j=j: field_kernel(g, j, *refs),
            "field_grad",
            [(wide_shape, F32)],
            arrived[j * g.pairs : (j + 1) * g.pairs] + [rows_of_kernel],
            flops=flops // 2,
        )[0]
        for j in range(2)
    ]
    stats, _, received = over_z("add_stats", stats, send, 1, ())
    hidden_shape = ((g.outer, count, g.gp, g.cells), BF16)
    normed, hidden, inv, sums, grad, send = call(
        g,
        norm_grad_kernel,
        "norm_grad",
        [rows_shape, hidden_shape, ((g.rb, g.cells), F32), stats_shape, rows_shape, sums_shape(2)],
        [rows, stats, gamma, beta] + fields + received,
        [pltpu.VMEM(*rows_shape), pltpu.VMEM((g.outer, g.gp, g.cells), BF16)],
    )
    half = g.outer // 2
    scratch = [
        pltpu.VMEM((half, g.used, g.gp, g.outs), F32),
        pltpu.VMEM((half, count, g.gp, wide_shape[-1]), BF16),
    ]
    near, far = call(
        g,
        sent_terms_kernel,
        "sent_terms",
        [packed_shape] * 2,
        arrived + [hidden],
        scratch,
        flops // 2,
    )
    sums, send, received = over_z("add_sums", sums, send, 1, [near])
    far = swap(far, g.inner)
    own, keep = call(
        g,
        kept_terms_kernel,
        "kept_terms",
        [((g.used * g.gp, g.outs), F32), ((g.sent, g.outs), F32)],
        arrived + [hidden],
        scratch,
        flops // 2,
        after=[send],
    )
    sends = call(
        g,
        finish_kernel,
        "finish",
        [block] * g.pairs,
        [sums, grad, normed, inv] + received,
        after=[own],
    )
    direct = [sends[0]] + [swap(sends[k], 2 * k) for k in range(1, g.pairs)]
    near = swap(pass_on(g, near, [send]), g.inner)
    (far,) = call(g, add_terms_kernel, "add_terms", [packed_shape], [keep, far], after=[near])
    terms = [near, swap(far, 2 * g.inner)]
    crossed = cross(g, "cross_grads", direct)
    d_acts, part = call(
        g,
        unpack_acts_kernel,
        "unpack_acts",
        [(acts.shape, BF16), ((g.per, STEP, g.outs), F32)],
        [own, terms[0]] + direct + [crossed],
        [pltpu.VMEM((g.used * g.gp, 128), F32)] * 2,
    )
    (d_weights,) = call(
        g, unpack_weights_kernel, "unpack_weights", [(weights.shape, F32)], [part] + terms[1:]
    )
    if g.blocks > 1:
        d_weights = lax.psum(d_weights, "block")
    return (d_acts, d_weights)


def solution(mesh):
    placed = (
        P("block", "tile", None, None),
        P(),
        P(),
        P("tile", None, None),
        P("block", "tile", None, None),
    )
    return jax.shard_map(
        shards,
        mesh=mesh,
        in_specs=placed,
        out_specs=(P("block", "tile", None, None), P("tile", None, None)),
        check_vma=False,
    )
```

```python
import jax
import jax.numpy as jnp
from jax import lax
from jax.experimental import pallas as pl
from jax.experimental.pallas import tpu as pltpu
from jax.sharding import PartitionSpec as P

GROUPS = 32
norm_eps = 1e-06


F32 = jnp.float32
BF16 = jnp.bfloat16
SPLIT = 16


class Sizes:
    def __init__(self, acts, weights, cotangent, tiles, blocks):
        self.frames, low_rows, self.cols, self.chans = acts.shape
        self.taps, self.outs = weights.shape[1:]
        self.tiles, self.blocks = tiles, blocks
        self.inner = 1 << (tiles.bit_length() // 2)
        self.outer = tiles // self.inner
        self.pairs = self.inner // 2
        self.per = self.chans // GROUPS
        self.gp = 16
        self.rb = self.outer * self.gp
        self.cells = self.frames * self.cols
        self.wide = 2 * self.cols
        self.grad_frames = self.frames * (2 if blocks > 1 else 1)
        self.first = max(0, 3 - self.frames * blocks)
        self.used = 9 * (3 - self.first)
        self.half = -(-self.used * self.per // 32) * 16
        self.sent = 2 * self.half
        self.wrows = self.sent + self.half
        self.lo = 128
        self.hi = self.outs - self.lo
        self.order = [*range(1, self.outer, 2), *range(0, self.outer, 2)]
        self.grows = 2 * self.grad_frames * self.outs
        self.count = float(low_rows * tiles * self.cols * self.per)
        if low_rows != 1 or tiles != GROUPS or self.hi != 64 or self.outer != 4:
            raise ValueError("unsupported sizes")


def swap(value, mask):
    count = lax.axis_size("tile")
    return lax.ppermute(value, "tile", [(i, i ^ mask) for i in range(count)])


def place(g):
    me = lax.axis_index("tile")
    return lax.div(me, g.inner), lax.rem(me, g.inner)


def iota(shape, dim):
    return lax.broadcasted_iota(jnp.int32, shape, dim)


def dot(a, b, dims=((1,), (0,))):
    return lax.dot_general(a, b, (dims, ((), ())), preferred_element_type=F32)


def channel_select(g, w, count):
    shape = (count * g.rb, g.chans)
    row = iota(shape, 0)
    block = row >> (g.rb.bit_length() - 1)
    group = (row & (g.rb - 1)) >> 4
    lane = row & (g.gp - 1)
    chan = g.per * (g.inner * group + (w ^ block)) + lane
    return (chan == iota(shape, 1)) & (lane < g.per)


def column_select(g):
    shape = (g.cells, g.frames * 3 * g.wide)
    row, col = iota(shape, 0), iota(shape, 1)
    bits = g.wide.bit_length() - 1
    part = col >> bits
    frame, shift = part, part
    frame = (part >= 3).astype(jnp.int32)
    for f in range(2, g.frames):
        frame = frame + (part >= 3 * f).astype(jnp.int32)
    shift = part - 3 * frame
    low = ((col & (g.wide - 1)) + shift - 1) >> 1
    inside = (low >= 0) & (low < g.cols)
    return (inside & (low + frame * g.cols == row)).astype(BF16)


def split(value, parts):
    out = []
    for _ in range(parts):
        piece = value.astype(BF16)
        out.append(piece)
        value = value - piece.astype(F32)
    return out


def sort_acts_kernel(g, acts_ref, *out_refs):
    _, w = place(g)
    pick = channel_select(g, w, g.inner).astype(BF16)
    blocks = dot(pick, acts_ref[...], ((1,), (1,))).astype(BF16)
    for k, ref in enumerate(out_refs):
        ref[...] = blocks[2 * k * g.rb : 2 * (k + 1) * g.rb].reshape(2, g.rb, g.cells)


def pack_rows(g, value):
    hi = jnp.concatenate([value[:, g.lo :], jnp.zeros((g.sent, 64), F32)], axis=1)
    lane = iota((g.half, 128), 1)
    both = jnp.where(lane < 64, hi[: g.half], pltpu.roll(hi[g.half :], 64, 1))
    return jnp.concatenate([value[:, : g.lo], both], axis=0).astype(BF16)


def unpack_rows(g, packed):
    both = packed[g.sent :].astype(F32)
    lane = iota(both.shape, 1)
    first = jnp.where(lane < 64, both, 0.0)
    second = jnp.where(lane < 64, pltpu.roll(both, 64, 1), 0.0)
    hi = jnp.concatenate([first, second], axis=0).astype(BF16)
    return jnp.concatenate([packed[: g.sent], hi], axis=1)


def pack_weights_kernel(g, weights_ref, out_ref):
    total = jnp.zeros((g.sent, g.outs), F32)
    row, tap = iota((g.sent, g.taps), 0), iota((g.sent, g.taps), 1) - 9 * g.first
    for i in range(g.per):
        pick = (row == tap * g.per + i) & (tap >= 0)
        total = total + dot(pick.astype(BF16), weights_ref[i])
    out_ref[...] = pack_rows(g, total)


def totals(g, first, second):
    pad = jnp.zeros((8 - g.outer, g.cells), F32)
    out = []
    for value in (first, second):
        out += [jnp.sum(value.reshape(g.outer, g.gp, g.cells), axis=1)]
        if g.outer < 8:
            out += [pad]
    return jnp.concatenate(out, axis=0)


def put_stats(ref, stats):
    for i, piece in enumerate(split(stats, 3)):
        ref[i * SPLIT : (i + 1) * SPLIT] = piece


def send_stats(g, ref, stats, z, rows_ref, parts):
    put_stats(ref, stats)
    last, even = rows_ref.shape[0] - 1, (z & 1) == 0
    for n, row in enumerate((jnp.where(even, last, 0), jnp.where(even, 0, last))):
        edge = rows_ref[row]
        for i, piece in enumerate(split(edge, parts) if parts > 1 else [edge.astype(BF16)]):
            at = 3 * SPLIT + (n * parts + i) * g.rb
            ref[at : at + g.rb] = piece


def step_kernel(g, stats_ref, received_ref, total_ref, send_ref):
    stats = add_stats(stats_ref[...], [received_ref])
    total_ref[...] = stats
    put_stats(send_ref, stats)
    count = send_ref.shape[0] - 3 * SPLIT
    send_ref[3 * SPLIT :] = received_ref[3 * SPLIT + count :]


def edges(g, z, received, parts):
    near, far = (
        sum(
            ref[3 * SPLIT + i * g.rb : 3 * SPLIT + (i + 1) * g.rb].astype(F32)
            for i in range(parts)
        )
        for ref in received
    )
    odd = (z & 1) == 1
    above = jnp.where(odd, near, jnp.where((z ^ 3) == z - 1, far, 0.0))
    below = jnp.where(odd, jnp.where((z ^ 3) == z + 1, far, 0.0), near)
    return above, below


def stats_kernel(g, *refs):
    direct, (crossed, rows_ref, stats_ref, send_ref) = refs[: g.pairs], refs[g.pairs :]
    z, w = place(g)
    first = jnp.zeros((g.rb, g.cells), F32)
    second = jnp.zeros((g.rb, g.cells), F32)
    for k in range(g.pairs):
        for j, block in enumerate((direct[k][0], crossed[k])):
            rows_ref[w ^ (2 * k + j)] = block
            wide = block.astype(F32)
            first = first + wide
            second = second + wide * wide
    stats = totals(g, first, second)
    stats_ref[...] = stats
    send_stats(g, send_ref, stats, z, rows_ref, 1)


def add_stats(own, received):
    for ref in received:
        for i in range(3):
            own = own + ref[i * SPLIT : (i + 1) * SPLIT].astype(F32)
    return own


def spread(g, stats):
    lane = iota((SPLIT, g.cells), 1)
    whole = jnp.zeros((SPLIT, g.cells), F32)
    for t in range(g.frames):
        mine = (lane >= t * g.cols) & (lane < (t + 1) * g.cols)
        part = jnp.sum(jnp.where(mine, stats, 0.0), axis=1, keepdims=True)
        whole = jnp.where(mine, part, whole)
    return tuple(
        jnp.concatenate(
            [
                jnp.broadcast_to(whole[s + q : s + q + 1], (g.gp, g.cells))
                for q in range(g.outer)
            ],
            axis=0,
        )
        for s in (0, 8)
    )


def prepare_weights_kernel(g, *refs):
    *packed, out_ref = refs
    z, _ = place(g)
    shape = (g.used * g.gp, g.sent)
    row, col = iota(shape, 0), iota(shape, 1)
    tap, lane = row >> 4, row & (g.gp - 1)
    pick = ((col == tap * g.per + lane) & (lane < g.per)).astype(BF16)
    blocks = [(ref, at) for ref in packed for at in range(0, ref.shape[0], g.wrows)]
    for k, (ref, at) in enumerate(blocks):
        value = dot(pick, unpack_rows(g, ref[at : at + g.wrows])).astype(BF16)
        out_ref[:, z ^ k] = value.reshape(g.used, g.gp, 256)


def meetings(g, later):
    pairs = [(a, later + a - 2) for a in range(g.first, 3)]
    return [(a, t) for a, t in pairs if 0 <= t < g.frames]


def fine_rows(g, ref, later):
    at = 2 * later * g.outs
    return jnp.concatenate([ref[at : at + g.outs], ref[at + g.outs : at + 2 * g.outs]], axis=1)


def lanes_of(g, t, e):
    return slice((3 * t + e) * g.wide, (3 * t + e + 1) * g.wide)


def field_kernel(g, j, *refs):
    *tiles, weights_ref, field = refs
    _, w = place(g)
    rb, wide = g.rb, g.wide
    field[...] = jnp.zeros_like(field)
    for k, ref in enumerate(tiles):
        row = w ^ (2 * k + j)
        for later in range(g.grad_frames):
            pairs = meetings(g, later)
            if not pairs:
                continue
            low, high = pairs[0][0] - g.first, pairs[-1][0] - g.first + 1
            taps = weights_ref[9 * low : 9 * high].reshape(9 * (high - low) * rb, 256)
            every = dot(taps[:, : g.outs], fine_rows(g, ref, later))
            for n, (_, t) in enumerate(pairs):
                back = every[9 * n * rb : 9 * (n + 1) * rb]
                part = lambda b, e, fine: back[
                    (3 * b + e) * rb : (3 * b + e + 1) * rb, fine * wide : (fine + 1) * wide
                ]
                for e in range(3):
                    lanes = lanes_of(g, t, e)
                    field[row, :, lanes] += part(0, e, 0)
                    field[row + 1, :, lanes] += (part(1, e, 0) + part(2, e, 0)) + (
                        part(0, e, 1) + part(1, e, 1)
                    )
                    field[row + 2, :, lanes] += part(2, e, 1)


def norm_grad_kernel(g, *refs):
    rows_ref, stats_ref, gamma_ref, beta_ref, field_ref, other_ref, *refs = refs
    received, refs = refs[:2], refs[2:]
    normed_ref, hidden_ref, inv_ref, sums_ref, grad_ref, send_ref, slope_ref, hidden_scratch = refs
    z, w = place(g)
    rb = g.rb
    total, total_sq = spread(g, add_stats(stats_ref[...], received[1:]))
    mean = total / g.count
    inv = lax.rsqrt(total_sq / g.count - mean * mean + norm_eps)
    inv_ref[...] = inv
    pick = channel_select(g, w, 1)
    gamma = jnp.sum(jnp.where(pick, gamma_ref[...].reshape(1, g.chans), 0.0), axis=1, keepdims=True)
    beta = jnp.sum(jnp.where(pick, beta_ref[...].reshape(1, g.chans), 0.0), axis=1, keepdims=True)

    def activate(place_at, block, present):
        normed = (block.astype(F32) - mean) * inv
        shifted = normed * gamma + beta
        gate = jax.nn.sigmoid(shifted)
        normed_ref[place_at] = normed
        hidden = (shifted * gate * present).astype(BF16).reshape(g.outer, g.gp, g.cells)
        hidden_scratch[...] = hidden
        for at, k in enumerate(g.order):
            hidden_ref[at, place_at] = hidden_scratch[z ^ k]
        slope_ref[place_at] = gate * (1.0 + shifted * (1.0 - gate)) * gamma * present

    above, below = edges(g, z, received, 1)
    activate(0, above, jnp.where(z > 0, 1.0, 0.0))
    activate(g.inner + 1, below, jnp.where(z < g.outer - 1, 1.0, 0.0))

    @pl.loop(0, g.inner)
    def _(i):
        activate(i + 1, rows_ref[i], 1.0)

    count = g.inner + 2
    select = column_select(g)
    flat = (field_ref[...] + other_ref[...]).reshape(count * rb, g.frames * 3 * g.wide)
    pieces = split(flat, 2)
    act_grad = dot(pieces[0], select, ((1,), (1,))) + dot(pieces[1], select, ((1,), (1,)))
    grad = act_grad.reshape(count, rb, g.cells) * slope_ref[...]
    grad_ref[...] = grad
    sums = totals(g, jnp.sum(grad, axis=0), jnp.sum(grad * normed_ref[...], axis=0))
    sums_ref[...] = sums
    send_stats(g, send_ref, sums, z, grad_ref, 1)


def kernel_terms(g, first, direct, crossed, hidden_ref, acc, ups):
    _, w = place(g)
    part = acc.shape[0]
    flat = hidden_ref[first : first + part].reshape(-1, g.cells)
    ups[...] = dot(flat, column_select(g)).astype(BF16).reshape(ups.shape)
    started = set()
    for later in range(g.grad_frames):
        for a, t in meetings(g, later):
            left, right = [], []
            for k in range(g.pairs):
                for j, ref in enumerate((direct[k], crossed[k])):
                    row = w ^ (2 * k + j)
                    pieces = []
                    for group in range(part):
                        for upper, lower in ((0, 1), (1, 1), (1, 2)):
                            for e in range(3):
                                lanes = lanes_of(g, t, e)
                                sides = [ups[group, row + at, :, lanes] for at in (upper, lower)]
                                pieces.append(jnp.concatenate(sides, axis=1))
                    left.append(jnp.concatenate(pieces, axis=0))
                    right.append(fine_rows(g, ref, later))
            terms = dot(
                jnp.concatenate(left, axis=1), jnp.concatenate(right, axis=1), ((1,), (1,))
            ).reshape(part, 9, g.gp, g.outs)
            taps = slice(9 * (a - g.first), 9 * (a - g.first + 1))
            if a in started:
                acc[:, taps] += terms
            else:
                acc[:, taps] = terms
                started.add(a)


def sent_order(g):
    shape = (g.sent, g.used * g.gp)
    row, col = iota(shape, 0), iota(shape, 1)
    tap, lane = col >> 4, col & (g.gp - 1)
    return ((row == tap * g.per + lane) & (lane < g.per)).astype(BF16)


def sent_terms_kernel(g, *refs):
    direct, crossed, refs = refs[: g.pairs], refs[g.pairs : 2 * g.pairs], refs[2 * g.pairs :]
    hidden_ref, *sends, acc, ups = refs
    kernel_terms(g, 0, direct, crossed, hidden_ref, acc, ups)
    pick = sent_order(g)
    for i, ref in enumerate(sends):
        terms = acc[i].reshape(g.used * g.gp, g.outs).astype(BF16)
        ref[...] = pack_rows(g, dot(pick, terms))


def kept_terms_kernel(g, *refs):
    direct, crossed, refs = refs[: g.pairs], refs[g.pairs : 2 * g.pairs], refs[2 * g.pairs :]
    hidden_ref, own_ref, keep_ref, acc, ups = refs
    kernel_terms(g, g.outer // 2, direct, crossed, hidden_ref, acc, ups)
    own_ref[...] = acc[0].reshape(g.used * g.gp, g.outs)
    pick = sent_order(g)
    terms = acc[1].reshape(g.used * g.gp, g.outs)
    keep_ref[...] = sum(dot(pick, piece) for piece in split(terms, 2))


def add_terms_kernel(g, keep_ref, received_ref, send_ref):
    block = unpack_rows(g, received_ref[...]).astype(F32)
    send_ref[...] = pack_rows(g, keep_ref[...] + block[:, : g.outs])


def finish_kernel(g, *refs):
    sums_ref, grad_ref, normed_ref, inv_ref, *refs = refs
    received, sends = refs[:2], refs[2:]
    z, w = place(g)
    first, second = spread(g, add_stats(sums_ref[...], received[1:]))
    first, second = first / g.count, second / g.count
    inv = inv_ref[...]
    above, below = edges(g, z, received, 1)
    for k, ref in enumerate(sends):
        for j in range(2):
            row = w ^ (2 * k + j)
            grad = grad_ref[row + 1]
            grad = grad + jnp.where(row == 0, above, 0.0)
            grad = grad + jnp.where(row == g.inner - 1, below, 0.0)
            ref[j] = (inv * (grad - first - normed_ref[row + 1] * second)).astype(BF16)


STEP = 32


def in_order(g, received):
    shape = (g.per * STEP, g.sent)
    row, col = iota(shape, 0), iota(shape, 1)
    tap, lane = row & (STEP - 1), row >> 5
    pick = ((col == tap * g.per + lane) & (tap < g.used)).astype(BF16)
    return sum(dot(pick, unpack_rows(g, ref[: g.wrows])) for ref in received)


def unpack_acts_kernel(g, own_ref, near_ref, *refs):
    direct, (crossed, acts_ref, part_ref, low, high) = refs[: g.pairs], refs[g.pairs :]
    _, w = place(g)
    pick = channel_select(g, w, g.inner).astype(BF16)
    blocks = []
    for k in range(g.pairs):
        blocks += [direct[k][0], crossed[k]]
    d_acts = dot(jnp.concatenate(blocks, axis=0), pick, ((0,), (0,)))
    acts_ref[...] = d_acts.astype(BF16).reshape(acts_ref.shape)
    total = in_order(g, [near_ref])
    low[...] = own_ref[:, : g.lo]
    high[:, : g.hi] = own_ref[:, g.lo :]
    for i in range(g.per):
        at = pl.ds(i, g.used, stride=g.gp)
        there = total[i * STEP : i * STEP + g.used]
        part_ref[i, : g.used, : g.lo] = low[at, :] + there[:, : g.lo]
        part_ref[i, : g.used, g.lo :] = high[at, :][:, : g.hi] + there[:, g.lo : g.outs]


def unpack_weights_kernel(g, part_ref, *refs):
    *received, out_ref = refs
    total = in_order(g, received)
    for i in range(g.per):
        if g.first:
            out_ref[i, : 9 * g.first, :] = jnp.zeros((9 * g.first, g.outs), F32)
        there = total[i * STEP : i * STEP + g.used, : g.outs]
        out_ref[i, 9 * g.first :, :] = part_ref[i, : g.used, :] + there


def call(g, kernel, name, outs, args, scratch=(), flops=0, after=()):
    shapes = [jax.ShapeDtypeStruct(shape, kind) for shape, kind in outs]
    whole = pl.BlockSpec(memory_space=pltpu.VMEM)
    moved = sum(a.size * a.dtype.itemsize for a in list(args) + shapes)
    count = len(args)
    rest = count + len(after)
    return pl.pallas_call(
        lambda *refs: kernel(g, *refs[:count], *refs[rest:]),
        out_shape=shapes,
        in_specs=[whole] * count + [pl.BlockSpec(memory_space=pl.ANY)] * len(after),
        out_specs=[whole] * len(shapes),
        scratch_shapes=list(scratch),
        compiler_params=pltpu.CompilerParams(vmem_limit_bytes=48 * 1024 * 1024),
        cost_estimate=pl.CostEstimate(flops=flops, bytes_accessed=moved, transcendentals=0),
        name=name,
    )(*args, *after)


def copy_kernel(g, in_ref, out_ref):
    out_ref[...] = in_ref[...]


def join_kernel(g, *refs):
    *parts, out_ref = refs
    at = 0
    for ref in parts:
        out_ref[at : at + ref.shape[0]] = ref[...]
        at += ref.shape[0]


def pass_on(g, value, after):
    return call(g, copy_kernel, "pass_on", [(value.shape, value.dtype)], [value], after=after)[0]


def cross_kernel(g, *refs):
    *blocks, out_ref = refs
    for k, ref in enumerate(blocks):
        out_ref[k] = ref[1]


def cross(g, name, direct):
    shape = (g.pairs, g.rb, g.cells)
    (out,) = call(g, cross_kernel, name, [(shape, BF16)], direct)
    return swap(out, 1)


def shards(acts, gamma, beta, weights, cotangent):
    g = Sizes(acts, weights, cotangent, lax.axis_size("tile"), lax.axis_size("block"))
    if g.blocks > 1:
        pairs = [(i + 1, i) for i in range(g.blocks - 1)]
        following = lax.ppermute(cotangent, "block", pairs)
        cotangent = jnp.concatenate([cotangent, following], 0)
    count = g.inner + 2
    block = ((2, g.rb, g.cells), BF16)
    rows_shape = ((count, g.rb, g.cells), F32)
    stats_shape = ((SPLIT, g.cells), F32)
    packed_shape = ((g.wrows, 128), BF16)
    wide_shape = (count, g.rb, g.frames * 3 * g.wide)
    sums_shape = lambda edges: ((3 * SPLIT + edges * g.rb, 128), BF16)

    def over_z(name, stats, send, parts, after):
        near = swap(send, g.inner)
        outs = [stats_shape, sums_shape(parts)]
        total, send = call(g, step_kernel, name, outs, [stats, near], after=after)
        return total, send, [near, swap(send, 2 * g.inner)]

    packed = list(
        call(g, pack_weights_kernel, "pack_weights", [packed_shape], [weights], flops=6 * 10**9)
    )
    for bit in range(g.outer.bit_length() - 1):
        whole = packed[0]
        if bit:
            shape = ((g.wrows << bit, 128), BF16)
            (whole,) = call(g, join_kernel, "join_kernel_rows", [shape], packed)
        packed.append(swap(whole, g.inner << bit))
    sends = call(
        g,
        sort_acts_kernel,
        "sort_acts",
        [block] * g.pairs,
        [acts.reshape(g.cells, g.chans)],
        flops=2*10**9,
    )
    blocks = [sends[0]] + [swap(sends[k], 2 * k) for k in range(1, g.pairs)]
    blocks.append(cross(g, "cross_acts", blocks))
    turned = jnp.swapaxes(cotangent, 2, 3).reshape(g.grows, g.wide)
    direct = [turned] + [swap(turned, 2 * k) for k in range(1, g.pairs)]
    arrived = direct + [swap(v, 1) for v in direct]

    rows, stats, send = call(
        g,
        stats_kernel,
        "stats",
        [((g.inner, g.rb, g.cells), BF16), stats_shape, sums_shape(2)],
        blocks,
        flops=5*10**9,
    )
    kernel_shape = ((g.used, g.outer, g.gp, 256), BF16)
    (rows_of_kernel,) = call(g, prepare_weights_kernel, "kernel_rows", [kernel_shape], packed, flops=7*10**9)
    flops = 2 * 2 * g.inner * 9 * g.rb * 256 * 256 * g.grad_frames
    fields = [
        call(
            g,
            lambda g, *refs, j=j: field_kernel(g, j, *refs),
            "field_grad",
            [(wide_shape, F32)],
            arrived[j * g.pairs : (j + 1) * g.pairs] + [rows_of_kernel],
            flops=flops // 2,
        )[0]
        for j in range(2)
    ]
    stats, _, received = over_z("add_stats", stats, send, 1, ())
    hidden_shape = ((g.outer, count, g.gp, g.cells), BF16)
    normed, hidden, inv, sums, grad, send = call(
        g,
        norm_grad_kernel,
        "norm_grad",
        [rows_shape, hidden_shape, ((g.rb, g.cells), F32), stats_shape, rows_shape, sums_shape(2)],
        [rows, stats, gamma, beta] + fields + received,
        [pltpu.VMEM(*rows_shape), pltpu.VMEM((g.outer, g.gp, g.cells), BF16)],
    )
    half = g.outer // 2
    scratch = [
        pltpu.VMEM((half, g.used, g.gp, g.outs), F32),
        pltpu.VMEM((half, count, g.gp, wide_shape[-1]), BF16),
    ]
    near, far = call(
        g,
        sent_terms_kernel,
        "sent_terms",
        [packed_shape] * 2,
        arrived + [hidden],
        scratch,
        flops // 2,
    )
    sums, send, received = over_z("add_sums", sums, send, 1, [near])
    far = swap(far, g.inner)
    own, keep = call(
        g,
        kept_terms_kernel,
        "kept_terms",
        [((g.used * g.gp, g.outs), F32), ((g.sent, g.outs), F32)],
        arrived + [hidden],
        scratch,
        flops // 2,
        after=[send],
    )
    sends = call(
        g,
        finish_kernel,
        "finish",
        [block] * g.pairs,
        [sums, grad, normed, inv] + received,
        after=[own],
    )
    direct = [swap(sends[k], 2 * k) for k in range(g.pairs - 1, 0, -1)]
    direct = [sends[0]] + direct[::-1]
    near = swap(pass_on(g, near, [send]), g.inner)
    (far,) = call(g, add_terms_kernel, "add_terms", [packed_shape], [keep, far], after=[near])
    terms = [near, swap(far, 2 * g.inner)]
    crossed = cross(g, "cross_grads", direct)
    d_acts, part = call(
        g,
        unpack_acts_kernel,
        "unpack_acts",
        [(acts.shape, BF16), ((g.per, STEP, g.outs), F32)],
        [own, terms[0]] + direct + [crossed],
        [pltpu.VMEM((g.used * g.gp, 128), F32)] * 2,
    )
    (d_weights,) = call(
        g, unpack_weights_kernel, "unpack_weights", [(weights.shape, F32)], [part] + terms[1:]
    )
    if g.blocks > 1:
        d_weights = lax.psum(d_weights, "block")
    return (d_acts, d_weights)


def solution(mesh):
    placed = (
        P("block", "tile", None, None),
        P(),
        P(),
        P("tile", None, None),
        P("block", "tile", None, None),
    )
    return jax.shard_map(
        shards,
        mesh=mesh,
        in_specs=placed,
        out_specs=(P("block", "tile", None, None), P("tile", None, None)),
        check_vma=False,
    )
```
